512 devices in a mesh: seq: 64 (over z, y), head: 8 (over x, core).
Axes of the slice: x: 4, y: 8, z: 8, core: 2. Of those that a mesh axis runs over, the one named last changes fastest.
Arguments:
- query_elements: bfloat16 [65536, 4096], P('seq', 'head'), may hold values from -4 to 4
- query_exponents: int32 [65536, 128], P('seq', 'head'), may hold values from -1 to 1
- key_elements: bfloat16 [65536, 512], P('seq', 'head'), may hold values from -4 to 4
- key_exponents: int32 [65536, 16], P('seq', 'head'), may hold values from -1 to 1
- value_elements: bfloat16 [65536, 512], P('seq', 'head'), may hold values from -4 to 4
- value_exponents: int32 [65536, 16], P('seq', 'head'), may hold values from -1 to 1
- query_clip_words: int32 [65536, 256], P('seq', 'head'), may hold values from 0 to 65280, as said below
- key_clip_words: int32 [65536, 32], P('seq', 'head'), may hold values from 0 to 65280, as said below
- sinks: float32 [64], P('head'), may hold values from -2 to 2
- rotation: float32 [8, 64, 64], P('head'), may hold values from -0.75 to 0.75
- output_gradient: bfloat16 [65536, 4096], P('seq', 'head'), may hold values from -120 to 120
Outputs:
- grad_q: bfloat16 [65536, 4096], P('seq', 'head')
- key_gradient_raw: bfloat16 [65536, 512], P('seq', 'head')
- value_gradient: bfloat16 [65536, 512], P('seq', 'head')
- grad_rotation: float32 [8, 64, 64], P('head')
- grad_sinks: float32 [64], P('head')
The draws below stay inside these ranges and needn't reach their ends.
Inputs may be any that keep to these rules, and one draw needn't show every extreme that they name: `query_clip_words`: bit b of word w of a row is 1 where entry 16 w + b of the row passed the clip; a word whose upper eight bits are all set has its lower eight bits clear. `key_clip_words`: bit b of word w of a row is 1 where entry 16 w + b of the row passed the clip; a word whose upper eight bits are all set has its lower eight bits clear.
All inputs are finite; a program needn't handle non-finite values.
Results may differ from the reference program's by a relative error of at most 0.0097.
Values may be sent and summed in bfloat16 or wider, within the bound.
A program may use at most 64 MiB of HBM per device.

```python
import math
import jax
import jax.numpy as jnp
from jax import lax

HEAD_ENTRIES = 64
KEY_VALUE_HEADS = 8
QUERY_PER_GROUP = 8
WINDOW = 128
SHARED_EXPONENT = 32
HQ = 64
SEQUENCE_TOKENS = 65536


def draw_query_elements(key, part):
    local_key = jax.random.fold_in(key, 11)
    final_result = jnp.clip(jax.random.normal(local_key, (SEQUENCE_TOKENS, HQ * HEAD_ENTRIES), jnp.float32), -4.0, 4.0)
    return final_result.astype(jnp.bfloat16)


def draw_key_elements(key, part):
    local_key = jax.random.fold_in(key, 12)
    final_result = jnp.clip(jax.random.normal(local_key, (SEQUENCE_TOKENS, KEY_VALUE_HEADS * HEAD_ENTRIES), jnp.float32), -4.0, 4.0)
    return final_result.astype(jnp.bfloat16)


def draw_output_gradient(key, part):
    positions = jnp.arange(SEQUENCE_TOKENS, dtype=jnp.float32)
    head_list = jnp.arange(HQ * HEAD_ENTRIES, dtype=jnp.int32) // HEAD_ENTRIES
    head_groups = (head_list // QUERY_PER_GROUP).astype(jnp.float32)
    head_spreading = 10.0 ** (0.5 * jax.random.uniform(jax.random.fold_in(key, 21), (HQ,), jnp.float32))
    column_factor = 3.0 ** (head_groups / max(KEY_VALUE_HEADS - 1, 1)) * head_spreading[head_list]
    row_scale = 3.0 ** (positions / max(SEQUENCE_TOKENS - 1, 1))
    local_key = jax.random.fold_in(key, 22)
    base_values = jnp.clip(jax.random.normal(local_key, (SEQUENCE_TOKENS, HQ * HEAD_ENTRIES), jnp.float32), -4.0, 4.0)
    return (base_values * row_scale[:, None] * column_factor[None, :]).astype(jnp.bfloat16)


def capped_flags(key, first_tag, second_tag, width):
    first_bits = jax.random.randint(jax.random.fold_in(key, first_tag), (SEQUENCE_TOKENS, width), 0, 65536, dtype=jnp.int32)
    second_bits = jax.random.randint(jax.random.fold_in(key, second_tag), (SEQUENCE_TOKENS, width), 0, 65536, dtype=jnp.int32)
    joined = jnp.bitwise_or(first_bits, second_bits)
    upper_full = jnp.bitwise_and(joined, 65280) == 65280
    return jnp.where(upper_full, jnp.bitwise_and(joined, 65280), joined)


def draw_query_clip_words(key, part):
    return capped_flags(key, 31, 32, HQ * HEAD_ENTRIES // 16)


def draw_key_clip_words(key, part):
    return capped_flags(key, 41, 42, KEY_VALUE_HEADS * HEAD_ENTRIES // 16)


def place_ends(drawn, key, least, largest):
    extent = drawn.shape
    place = [jax.random.randint(jax.random.fold_in(key, axis), (), 0, extent[axis]) for axis in range(len(extent))]
    drawn = drawn.at[tuple(place)].set(least)
    longest = extent.index(max(extent))
    place[longest] = (place[longest] + 1) % extent[longest]
    return drawn.at[tuple(place)].set(largest)


def levels(stream_key, extent, split, low, largest):
    level = 1.0
    for axis_at, shards_of in split:
        steps = jax.random.uniform(jax.random.fold_in(jax.random.fold_in(stream_key, 6), axis_at), (shards_of,), jnp.float32, low / len(split), largest / len(split))
        level = level * jnp.repeat(jnp.exp(steps), extent[axis_at] // shards_of).reshape((-1,) + (1,) * (len(extent) - 1 - axis_at))
    return level


def noise(rng, shape, scale, bound, pieces=(), held_as=jnp.bfloat16):
    array = scale * jax.random.normal(rng, shape, jnp.float32)
    if pieces:
        array = array * levels(rng, shape, pieces, -0.22, 0.18)
    return jnp.clip(array, -bound, bound).astype(held_as)


def setup_inputs(seed: int = 0) -> dict:
    key_list = jax.random.split(jax.random.key(seed), 12)
    query_elements = draw_query_elements(jax.random.fold_in(key_list[11], 71), 0)
    query_exponents = place_ends(jax.random.randint(key_list[1], (SEQUENCE_TOKENS, HQ * HEAD_ENTRIES // SHARED_EXPONENT), -1, 2), jax.random.fold_in(key_list[1], 1), -1, 1).astype(jnp.int32)
    key_elements = draw_key_elements(jax.random.fold_in(key_list[11], 71), 0)
    key_exponents = place_ends(jax.random.randint(key_list[3], (SEQUENCE_TOKENS, KEY_VALUE_HEADS * HEAD_ENTRIES // SHARED_EXPONENT), -1, 2), jax.random.fold_in(key_list[3], 1), -1, 1).astype(jnp.int32)
    value_elements = noise(key_list[4], (SEQUENCE_TOKENS, KEY_VALUE_HEADS * HEAD_ENTRIES), 1.0, 4.0, ((0, 64), (1, 8)))
    value_exponents = place_ends(jax.random.randint(key_list[5], (SEQUENCE_TOKENS, KEY_VALUE_HEADS * HEAD_ENTRIES // SHARED_EXPONENT), -1, 2), jax.random.fold_in(key_list[5], 1), -1, 1).astype(jnp.int32)
    query_clip_words = draw_query_clip_words(jax.random.fold_in(key_list[11], 71), 0)
    key_clip_words = draw_key_clip_words(jax.random.fold_in(key_list[11], 71), 0)
    sinks = jnp.clip(jax.random.uniform(key_list[8], (HQ,), jnp.float32, -2.0, 2.0) * levels(key_list[8], (HQ,), ((0, 8),), -0.4, 0.0), -2.0, 2.0)
    rotation = noise(key_list[9], (KEY_VALUE_HEADS, HEAD_ENTRIES, HEAD_ENTRIES), HEAD_ENTRIES ** -0.5, 0.75, ((0, 8),), jnp.float32)
    output_gradient = draw_output_gradient(jax.random.fold_in(key_list[11], 71), 0)
    return dict(query_elements=query_elements, query_exponents=query_exponents, key_elements=key_elements, key_exponents=key_exponents, value_elements=value_elements, value_exponents=value_exponents, query_clip_words=query_clip_words, key_clip_words=key_clip_words, sinks=sinks, rotation=rotation, output_gradient=output_gradient)


clip_scale = 64.0
limit_factor = 0.05
negative = -1e+30

def decode_blocks(element_vals, powers):
    row_count = element_vals.shape[0]
    scaled = element_vals.astype(jnp.float32).reshape(row_count, -1, SHARED_EXPONENT) * jnp.exp2(powers.astype(jnp.float32))[:, :, None]
    return scaled.reshape(row_count, -1).astype(jnp.bfloat16)

def unpack_words(packed):
    shifts = jnp.arange(16, dtype=jnp.int32)
    bit_vals = jnp.right_shift(packed[:, :, None], shifts[None, None, :]) & 1
    return bit_vals.reshape(packed.shape[0], -1).astype(jnp.float32)

def attend(query_blk, dout_blk, keys_blk, values, sink_logit, query_pos, key_pos):
    temper = HEAD_ENTRIES ** (-0.5)
    query_f = query_blk.astype(jnp.float32)
    dout_f = dout_blk.astype(jnp.float32)
    keys_f = keys_blk.astype(jnp.float32)
    values_f = values.astype(jnp.float32)
    scores = jnp.einsum('iqd,jd->qij', query_f, keys_f) * temper
    allowed = (key_pos[None, :] <= query_pos[:, None]) & (key_pos[None, :] > query_pos[:, None] - WINDOW) & (key_pos[None, :] >= 0)
    scores = jnp.where(allowed[None], scores, negative)
    row_max = jnp.maximum(lax.optimization_barrier(jnp.max(scores, axis=2)), sink_logit[:, None])
    numerators = jnp.where(allowed[None], jnp.exp(scores - row_max[:, :, None]), 0.0)
    totals = lax.optimization_barrier(jnp.sum(numerators, axis=2)) + jnp.exp(sink_logit[:, None] - row_max)
    weights = numerators / totals[:, :, None]
    rounded = weights.astype(jnp.bfloat16).astype(jnp.float32)
    outputs = jnp.einsum('qij,jd->iqd', rounded, values_f)
    deltas = lax.optimization_barrier(jnp.sum(dout_f * outputs, axis=2)).T
    grad_probs = jnp.einsum('iqd,jd->qij', dout_f, values_f)
    grad_scores = (weights * (grad_probs - deltas[:, :, None])).astype(jnp.bfloat16).astype(jnp.float32)
    grad_query = jnp.einsum('qij,jd->iqd', grad_scores, keys_f) * temper
    grad_keys = jnp.einsum('qij,iqd->jd', grad_scores, query_f) * temper
    grad_vals = jnp.einsum('qij,iqd->jd', rounded, dout_f)
    sink_terms = -lax.optimization_barrier(jnp.sum(jnp.exp(sink_logit[:, None] - row_max) / totals * deltas, axis=1))
    return (grad_query, grad_keys, grad_vals, sink_terms)

def reference(query_elements, query_exponents, key_elements, key_exponents, value_elements, value_exponents, query_clip_words, key_clip_words, sinks, rotation, output_gradient):
    query_rows_list = decode_blocks(query_elements, query_exponents).reshape(SEQUENCE_TOKENS, KEY_VALUE_HEADS, QUERY_PER_GROUP, HEAD_ENTRIES).transpose(1, 0, 2, 3)
    key_row_list = decode_blocks(key_elements, key_exponents).reshape(SEQUENCE_TOKENS, KEY_VALUE_HEADS, HEAD_ENTRIES).transpose(1, 0, 2)
    value_row_list = decode_blocks(value_elements, value_exponents).reshape(SEQUENCE_TOKENS, KEY_VALUE_HEADS, HEAD_ENTRIES).transpose(1, 0, 2)
    output_grad_list = output_gradient.reshape(SEQUENCE_TOKENS, KEY_VALUE_HEADS, QUERY_PER_GROUP, HEAD_ENTRIES).transpose(1, 0, 2, 3)
    query_flags = unpack_words(query_clip_words).reshape(SEQUENCE_TOKENS, KEY_VALUE_HEADS, QUERY_PER_GROUP, HEAD_ENTRIES).transpose(1, 0, 2, 3)
    key_flags = unpack_words(key_clip_words).reshape(SEQUENCE_TOKENS, KEY_VALUE_HEADS, HEAD_ENTRIES).transpose(1, 0, 2)
    sink_row_list = sinks.reshape(KEY_VALUE_HEADS, QUERY_PER_GROUP)
    block_count = SEQUENCE_TOKENS // WINDOW

    def group(items):
        query_g, key_g, value_g, dout_g, qbit_g, kbit_g, sink_g, rot_g = items
        zero_rows = jnp.zeros((WINDOW, HEAD_ENTRIES), jnp.bfloat16)
        key_pad = jnp.concatenate([zero_rows, key_g], 0)
        value_pad = jnp.concatenate([zero_rows, value_g], 0)

        def block(block_index):
            begin_row = block_index * WINDOW
            query_b = lax.dynamic_slice_in_dim(query_g, begin_row, WINDOW, 0)
            dout_b = lax.dynamic_slice_in_dim(dout_g, begin_row, WINDOW, 0)
            keys_b = lax.dynamic_slice_in_dim(key_pad, begin_row, 2 * WINDOW, 0)
            values_b = lax.dynamic_slice_in_dim(value_pad, begin_row, 2 * WINDOW, 0)
            query_pos = begin_row + jnp.arange(WINDOW, dtype=jnp.int32)
            key_pos = begin_row - WINDOW + jnp.arange(2 * WINDOW, dtype=jnp.int32)
            return attend(query_b, dout_b, keys_b, values_b, sink_g, query_pos, key_pos)
        grad_query, grad_keys, grad_vals, sink_terms = lax.map(block, jnp.arange(block_count, dtype=jnp.int32))
        zero_tail = jnp.zeros((1, WINDOW, HEAD_ENTRIES), jnp.float32)
        key_total = grad_keys[:, WINDOW:] + jnp.concatenate([grad_keys[1:, :WINDOW], zero_tail], 0)
        value_total = grad_vals[:, WINDOW:] + jnp.concatenate([grad_vals[1:, :WINDOW], zero_tail], 0)
        grad_query = grad_query.reshape(SEQUENCE_TOKENS, QUERY_PER_GROUP, HEAD_ENTRIES)
        key_total = key_total.reshape(SEQUENCE_TOKENS, HEAD_ENTRIES)
        value_total = value_total.reshape(SEQUENCE_TOKENS, HEAD_ENTRIES)
        masked_query = (grad_query * qbit_g).astype(jnp.bfloat16)
        masked_keys = (key_total * kbit_g).astype(jnp.bfloat16)
        rotation_low = rot_g.astype(jnp.bfloat16)
        grad_query_pre = jnp.einsum('tqd,ed->tqe', masked_query.astype(jnp.float32), rotation_low.astype(jnp.float32)).astype(jnp.bfloat16)
        grad_key_pre = jnp.dot(masked_keys, rotation_low.T, preferred_element_type=jnp.float32).astype(jnp.bfloat16)
        partial_value = jnp.dot(query_g.reshape(-1, HEAD_ENTRIES).T, masked_query.reshape(-1, HEAD_ENTRIES), preferred_element_type=jnp.float32)
        partial_value = partial_value + jnp.dot(key_g.T, masked_keys, preferred_element_type=jnp.float32)
        raw_grad = jnp.dot(rot_g, partial_value, precision=lax.Precision.HIGHEST)
        return (grad_query_pre, grad_key_pre, value_total.astype(jnp.bfloat16), raw_grad, lax.optimization_barrier(jnp.sum(sink_terms, axis=0)))
    grad_query_all, every_key_gradient, every_value_gradient, raw_all, sink_all = lax.map(group, (query_rows_list, key_row_list, value_row_list, output_grad_list, query_flags, key_flags, sink_row_list, rotation))
    limit_value = limit_factor * math.sqrt(SEQUENCE_TOKENS * HQ * HEAD_ENTRIES)
    norm_value = jnp.sqrt(jnp.sum(raw_all * raw_all))
    grad_rotation = raw_all * (clip_scale / jnp.maximum(norm_value, limit_value))
    grad_q = grad_query_all.transpose(1, 0, 2, 3).reshape(SEQUENCE_TOKENS, HQ * HEAD_ENTRIES)
    key_gradient_raw = every_key_gradient.transpose(1, 0, 2).reshape(SEQUENCE_TOKENS, KEY_VALUE_HEADS * HEAD_ENTRIES)
    value_gradient = every_value_gradient.transpose(1, 0, 2).reshape(SEQUENCE_TOKENS, KEY_VALUE_HEADS * HEAD_ENTRIES)
    return (grad_q, key_gradient_raw, value_gradient, grad_rotation, sink_all.reshape(HQ))
```

```python
import functools
import math

import jax
import jax.numpy as jnp
from jax import lax
from jax.experimental import pallas as pl
from jax.experimental.pallas import tpu as pltpu
from jax.sharding import PartitionSpec as P

WINDOW = 128
HEAD = 64
PAIR = 2 * HEAD
clip_scale = 64.0
limit_factor = 0.05
temper = 0.125
negative = -1e30
f32 = jnp.float32
bf16 = jnp.bfloat16
MESH = pl.DeviceIdType.MESH

NN = (((1,), (0,)), ((), ()))
NT = (((1,), (1,)), ((), ()))


def mm(a, b, dims=NN):
    return lax.dot_general(a, b, dims, preferred_element_type=f32)


def spread(ref, first, count, times, cols):
    width = WINDOW
    return jnp.concatenate(
        [jnp.broadcast_to(ref[first + r : first + r + 1, cols], (times, width)) for r in range(count)], axis=0
    )


def kernel(sizes, limit_value, *refs):
    (
        qe_hbm, qx_hbm, kt_hbm, kx_hbm, vt_hbm, vx_hbm, qc_hbm, kc_hbm, sinks, rot_hbm, do_hbm,
        gq_hbm, gk_hbm, gv_hbm, gr_hbm, gs_hbm,
        q_s, d_s, g_s, qx_s, kt_s, kx_s, vt_s, vx_s, qc_s, kc_s, rot_s,
        scale_s, kv_t, k_row, v_row, dkv, rb_s, part_s, sinkacc, tri_s, back_in, gk_s, gv_s,
        buf_a1, buf_b1, buf_a2, buf_b2, sq_buf, gr_s, gs_s,
        q_sem, d_sem, g_sem, in_sem, out_sem, halo_sem, back_sem,
        a1_send, a1_recv, b1_send, b1_recv, a2_send, a2_recv, b2_send, b2_recv, h_send, h_recv,
    ) = refs
    nz, ny, nh, blocks, heads = sizes
    ns = nz * ny
    pairs = heads // 2
    me_s = lax.axis_index("seq")
    me_h = lax.axis_index("head")
    me_z, me_y = me_s // ny, lax.rem(me_s, ny)
    nxt, prv = lax.rem(me_s + 1, ns), lax.rem(me_s + ns - 1, ns)

    def seq_dev(s):
        return (s, me_h)

    z_peers = [(lax.rem(me_z + k, nz)) for k in range(1, nz)]
    y_peers = [(lax.rem(me_y + k, ny)) for k in range(1, ny)]
    h_peers = [(lax.rem(me_h + k, nh)) for k in range(1, nh)]

    barrier = pltpu.get_barrier_semaphore()
    targets = [(nxt, me_h), (prv, me_h)]
    targets += [(z * ny + me_y, me_h) for z in z_peers]
    targets += [(me_z * ny + y, me_h) for y in y_peers]
    targets += [(me_s, h) for h in h_peers]
    for dev in targets:
        pl.semaphore_signal(barrier, inc=1, device_id=dev, device_id_type=MESH)

    small = [
        (kt_hbm, kt_s), (kx_hbm, kx_s), (vt_hbm, vt_s), (vx_hbm, vx_s),
        (qx_hbm, qx_s), (qc_hbm, qc_s), (kc_hbm, kc_s), (rot_hbm, rot_s),
    ]
    small_copies = [pltpu.make_async_copy(a, b, in_sem.at[n]) for n, (a, b) in enumerate(small)]
    for c in small_copies[:4]:
        c.start()

    def q_copy(b):
        rows = pl.ds(pl.multiple_of(b * WINDOW, WINDOW), WINDOW)
        return pltpu.make_async_copy(qe_hbm.at[rows], q_s.at[rows], q_sem.at[b])

    def d_copy(b):
        rows = pl.ds(pl.multiple_of(b * WINDOW, WINDOW), WINDOW)
        return pltpu.make_async_copy(do_hbm.at[rows], d_s.at[rows], d_sem.at[b])

    def g_copy(b):
        rows = pl.ds(pl.multiple_of(b * WINDOW, WINDOW), WINDOW)
        return pltpu.make_async_copy(g_s.at[rows], gq_hbm.at[rows], g_sem.at[b])

    def at_step(n):
        return jnp.where(n < 5, n + 1, jnp.where(n == 5, 0, n))

    for n in range(blocks):
        b = [1, 2, 3, 4, 5, 0, 6, 7][n]
        q_copy(b).start()
        d_copy(b).start()
        if n == 0:
            for c in small_copies[4:]:
                c.start()

    p_iota = lax.broadcasted_iota(jnp.int32, (WINDOW, 2 * WINDOW), 0)
    i_iota = lax.rem(lax.broadcasted_iota(jnp.int32, (WINDOW, 2 * WINDOW), 1), WINDOW)
    tri_s[...] = jnp.where(p_iota <= i_iota, 1.0, 0.0).astype(bf16)
    part_s[...] = jnp.zeros_like(part_s)
    sinkacc[...] = jnp.zeros_like(sinkacc)
    dkv[...] = jnp.zeros_like(dkv)

    for c in small_copies[:4]:
        c.wait()
    ksc = jnp.exp2(kx_s[...].astype(f32)) * temper
    vsc = jnp.exp2(vx_s[...].astype(f32))
    for half in range(2):
        rr = slice(32 * half, 32 * half + 32)
        k8 = (kt_s[rr, :].astype(f32) * ksc[half : half + 1, :]).astype(bf16)
        vv = (vt_s[rr, :].astype(f32) * vsc[half : half + 1, :]).astype(bf16)
        kv_t[32 * half : 32 * half + 32, WINDOW:] = k8
        kv_t[HEAD + 32 * half : HEAD + 32 * half + 32, WINDOW:] = vv

    def rows_of(cb):
        at = pl.ds(pl.multiple_of(cb * WINDOW, WINDOW), WINDOW)
        both = kv_t[:, at]
        k_row[at, :] = both[:HEAD].T
        v_row[at, :] = both[HEAD:].T

    def rows_step(cb, carry):
        rows_of(cb)
        return carry

    lax.fori_loop(1, blocks + 1, rows_step, 0)

    for c in small_copies[4:]:
        c.wait()
    scale_s[...] = jnp.exp2(qx_s[...].astype(f32))
    rlow = rot_s[...].astype(bf16)
    rlow_t = rot_s[...].T.astype(bf16)
    zero = jnp.zeros((HEAD, HEAD), bf16)
    rb_s[...] = jnp.concatenate(
        [jnp.concatenate([rlow_t, zero], axis=1), jnp.concatenate([zero, rlow_t], axis=1)], axis=0
    )

    halo = pltpu.make_async_remote_copy(
        src_ref=kv_t.at[:, pl.ds(blocks * WINDOW, WINDOW)],
        dst_ref=kv_t.at[:, pl.ds(0, WINDOW)],
        send_sem=halo_sem.at[0], recv_sem=halo_sem.at[1],
        device_id=(nxt, me_h), device_id_type=MESH,
    )
    back = pltpu.make_async_remote_copy(
        src_ref=dkv.at[:, pl.ds(0, WINDOW)],
        dst_ref=back_in,
        send_sem=back_sem.at[0], recv_sem=back_sem.at[1],
        device_id=(prv, me_h), device_id_type=MESH,
    )
    bits = jnp.left_shift(1, lax.broadcasted_iota(jnp.int32, (16, WINDOW), 0))
    bits64 = jnp.concatenate([bits] * 4, axis=0)

    def step(n, carry):
        b = at_step(n)

        @pl.when(n == 3)
        def _():
            pl.semaphore_wait(barrier, len(targets))
            halo.start()

        @pl.when(n == 5)
        def _():
            halo.wait()
            rows_of(0)

        q_copy(b).wait()
        d_copy(b).wait()
        cols = pl.ds(pl.multiple_of(b * WINDOW, WINDOW), WINDOW)
        wide = pl.ds(pl.multiple_of(b * WINDOW, WINDOW), 2 * WINDOW)
        hidden = jnp.where((b == 0) & (me_s == 0), negative, 0.0)
        k2 = k_row[wide, :]
        v2 = v_row[wide, :]
        k2t = kv_t[:HEAD, wide]
        dk = jnp.zeros((HEAD, 2 * WINDOW), f32)
        dv = jnp.zeros((HEAD, 2 * WINDOW), f32)
        part = jnp.zeros((HEAD, HEAD), f32)
        tri = p_iota <= i_iota
        for pr in range(pairs):
            lanes = slice(pr * PAIR, (pr + 1) * PAIR)
            qt = q_s[cols, lanes].T * spread(scale_s, 4 * pr, 4, 32, cols).astype(bf16)
            dt = d_s[cols, lanes].T
            q2 = jnp.concatenate([qt[:HEAD], qt[HEAD:]], axis=1)
            d2 = jnp.concatenate([dt[:HEAD], dt[HEAD:]], axis=1)
            s_all = mm(k2, q2)
            s = jnp.where(tri, s_all[WINDOW:], s_all[:WINDOW] + hidden)
            sink = jnp.concatenate(
                [jnp.full((1, WINDOW), sinks[2 * pr + h], f32) for h in range(2)], axis=1
            )
            top = jnp.maximum(jnp.max(s, axis=0, keepdims=True), sink)
            e = jnp.exp(s - top)
            es = jnp.exp(sink - top)
            inv = 1.0 / (jnp.sum(e, axis=0, keepdims=True) + es)
            w = e * inv
            dp_all = mm(v2, d2)
            dp = jnp.where(tri, dp_all[WINDOW:], dp_all[:WINDOW])
            t = w * dp
            delta = jnp.sum(t, axis=0, keepdims=True)
            ds = t - w * delta
            sk = es * inv * delta
            sinkacc[2 * pr : 2 * pr + 1, :] -= sk[:, :WINDOW]
            sinkacc[2 * pr + 1 : 2 * pr + 2, :] -= sk[:, WINDOW:]
            wb = w.astype(bf16)
            sb = ds.astype(bf16)
            trib = tri_s[...]
            w_cur = wb * trib
            s_cur = sb * trib
            w2 = jnp.concatenate([wb - w_cur, w_cur], axis=0)
            s2 = jnp.concatenate([sb - s_cur, s_cur], axis=0)
            dv = dv + mm(d2, w2, NT)
            dk = dk + mm(q2, s2, NT)
            gqt = mm(k2t, s2)
            m2 = []
            for h in range(2):
                words = spread(qc_s, 4 * (2 * pr + h), 4, 16, cols)
                keep = jnp.bitwise_and(words, bits64) != 0
                m2.append(jnp.where(keep, gqt[:, h * WINDOW : (h + 1) * WINDOW], 0.0).astype(bf16))
            part = part + mm(q2, jnp.concatenate(m2, axis=1), NT)
            rows_q = jnp.concatenate(m2, axis=0).T
            g_s[cols, lanes] = mm(rows_q, rb_s[...]).astype(bf16)
        dkv[:HEAD, wide] += dk
        dkv[HEAD:, wide] += dv
        part_s[...] += part
        g_copy(b).start()

        @pl.when(n == 5)
        def _():
            back.start()

        return carry

    lax.fori_loop(0, blocks, step, 0)
    back.wait()

    last = pl.ds(blocks * WINDOW, WINDOW)
    dkv[:, last] += back_in[...]

    def key_step(cb, carry):
        at = pl.ds(pl.multiple_of(cb * WINDOW, WINDOW), WINDOW)
        ext = pl.ds(pl.multiple_of((cb + 1) * WINDOW, WINDOW), WINDOW)
        keep = jnp.bitwise_and(spread(kc_s, 0, 4, 16, at), bits64) != 0
        mk = jnp.where(keep, dkv[:HEAD, ext] * temper, 0.0).astype(bf16)
        gk_s[:, at] = mm(rlow, mk).astype(bf16)
        gv_s[:, at] = dkv[HEAD:, ext].astype(bf16)
        part_s[...] += mm(kv_t[:HEAD, ext], mk, NT) * (1.0 / temper)
        return carry

    lax.fori_loop(0, blocks, key_step, 0)
    gk_copy = pltpu.make_async_copy(gk_s, gk_hbm, out_sem.at[0])
    gv_copy = pltpu.make_async_copy(gv_s, gv_hbm, out_sem.at[1])
    gk_copy.start()
    gv_copy.start()

    cut = buf_a1.shape[1]
    part = part_s[...]
    folded = jnp.concatenate([part[: HEAD // 2], part[HEAD // 2 :]], axis=1)
    buf_a1[pl.ds(me_z, 1)] = folded[:cut][None]
    buf_b1[pl.ds(me_y, 1)] = jnp.concatenate([folded[cut:], sinkacc[...]], axis=0)[None]

    def exchange(buf, me, peers, device, send, recv):
        copies = []
        for k, peer in enumerate(peers):
            copies.append(
                pltpu.make_async_remote_copy(
                    src_ref=buf.at[me], dst_ref=buf.at[me],
                    send_sem=send.at[k], recv_sem=recv.at[k],
                    device_id=device(peer), device_id_type=MESH,
                )
            )
        for c in copies:
            c.start()
        return copies

    def along_z(z):
        return (z * ny + me_y, me_h)

    def along_y(y):
        return (me_z * ny + y, me_h)

    def along_h(h):
        return (me_s, h)

    def total(buf, count):
        acc = buf[0]
        for k in range(1, count):
            acc = acc + buf[k]
        return acc

    copies_a = exchange(buf_a1, me_z, z_peers, along_z, a1_send, a1_recv)
    copies_b = exchange(buf_b1, me_y, y_peers, along_y, b1_send, b1_recv)
    for c in copies_a:
        c.wait()
    buf_a2[pl.ds(me_y, 1)] = total(buf_a1, nz)[None]
    copies_a = exchange(buf_a2, me_y, y_peers, along_y, a2_send, a2_recv)
    for c in copies_b:
        c.wait()
    buf_b2[pl.ds(me_z, 1)] = total(buf_b1, ny)[None]
    copies_b = exchange(buf_b2, me_z, z_peers, along_z, b2_send, b2_recv)
    for c in copies_a:
        c.wait()
    for c in copies_b:
        c.wait()
    tot_a = total(buf_a2, ny)
    tot_b = total(buf_b2, nz)
    rows_b = HEAD // 2 - cut
    whole = jnp.concatenate([tot_a, tot_b[:rows_b]], axis=0)
    summed = jnp.concatenate([whole[:, :HEAD], whole[:, HEAD:]], axis=0)
    raw = lax.dot_general(
        rot_s[...], summed, NN, precision=lax.Precision.HIGHEST, preferred_element_type=f32
    )
    sq = jnp.sum(jnp.sum(raw * raw, axis=0, keepdims=True), axis=1, keepdims=True)
    sq_buf[pl.ds(me_h, 1)] = jnp.broadcast_to(sq, (8, 128))[None]
    copies_h = exchange(sq_buf, me_h, h_peers, along_h, h_send, h_recv)
    gs_s[...] = jnp.sum(tot_b[rows_b:].T, axis=0, keepdims=True)
    gs_copy = pltpu.make_async_copy(gs_s, gs_hbm, out_sem.at[2])
    gs_copy.start()
    for c in copies_h:
        c.wait()
    norm = jnp.sqrt(total(sq_buf, nh)[:1, :HEAD])
    gr_s[...] = raw * (clip_scale / jnp.maximum(norm, limit_value))
    gr_copy = pltpu.make_async_copy(gr_s, gr_hbm, out_sem.at[3])
    gr_copy.start()

    def g_wait(b, carry):
        g_copy(b).wait()
        return carry

    lax.fori_loop(0, blocks, g_wait, 0)
    gk_copy.wait()
    gv_copy.wait()
    gs_copy.wait()
    gr_copy.wait()


def per_device(split, ns, nh, qe, qx, ke, kx, ve, vx, qc, kc, sinks, rot, dout):
    tokens, width = qe.shape
    heads = width // HEAD
    blocks = tokens // WINDOW
    nz, ny = split
    limit_value = limit_factor * math.sqrt(tokens * ns * heads * nh * HEAD)
    cut = 16
    rest = HEAD // 2 - cut + 8
    any_space = pl.BlockSpec(memory_space=pl.ANY)
    vmem = pltpu.VMEM
    dma = pltpu.SemaphoreType.DMA
    ext = tokens + WINDOW
    outs = pl.pallas_call(
        functools.partial(kernel, (nz, ny, nh, blocks, heads), limit_value),
        out_shape=(
            jax.ShapeDtypeStruct((tokens, width), bf16),
            jax.ShapeDtypeStruct((HEAD, tokens), bf16),
            jax.ShapeDtypeStruct((HEAD, tokens), bf16),
            jax.ShapeDtypeStruct((HEAD, HEAD), f32),
            jax.ShapeDtypeStruct((1, heads), f32),
        ),
        in_specs=[any_space] * 8 + [pl.BlockSpec(memory_space=pltpu.SMEM)] + [any_space] * 2,
        out_specs=(any_space,) * 5,
        scratch_shapes=[
            vmem((tokens, width), bf16),
            vmem((tokens, width), bf16),
            vmem((tokens, width), bf16),
            vmem((2 * heads, tokens), jnp.int32),
            vmem((HEAD, tokens), bf16),
            vmem((2, tokens), jnp.int32),
            vmem((HEAD, tokens), bf16),
            vmem((2, tokens), jnp.int32),
            vmem((4 * heads, tokens), jnp.int32),
            vmem((4, tokens), jnp.int32),
            vmem((HEAD, HEAD), f32),
            vmem((2 * heads, tokens), f32),
            vmem((2 * HEAD, ext), bf16),
            vmem((ext, HEAD), bf16),
            vmem((ext, HEAD), bf16),
            vmem((2 * HEAD, ext), f32),
            vmem((PAIR, PAIR), bf16),
            vmem((HEAD, HEAD), f32),
            vmem((heads, WINDOW), f32),
            vmem((WINDOW, 2 * WINDOW), bf16),
            vmem((2 * HEAD, WINDOW), f32),
            vmem((HEAD, tokens), bf16),
            vmem((HEAD, tokens), bf16),
            vmem((nz, cut, 128), f32),
            vmem((ny, rest, 128), f32),
            vmem((ny, cut, 128), f32),
            vmem((nz, rest, 128), f32),
            vmem((nh, 8, 128), f32),
            vmem((HEAD, HEAD), f32),
            vmem((1, heads), f32),
            dma((blocks,)),
            dma((blocks,)),
            dma((blocks,)),
            dma((8,)),
            dma((4,)),
            dma((2,)),
            dma((2,)),
            dma((nz,)), dma((nz,)), dma((ny,)), dma((ny,)),
            dma((ny,)), dma((ny,)), dma((nz,)), dma((nz,)),
            dma((nh,)), dma((nh,)),
        ],
        compiler_params=pltpu.CompilerParams(
            collective_id=0, has_side_effects=True, vmem_limit_bytes=63 * 1024 * 1024
        ),
    )(qe, qx.T, ke.T, kx.T, ve.T, vx.T, qc.T, kc.T, sinks, rot.reshape(HEAD, HEAD), dout)
    gq, gk, gv, gr, gs = outs
    return (gq, gk.T, gv.T, gr[None], gs.reshape(heads))


def solution(mesh):
    ns, nh = mesh.shape["seq"], mesh.shape["head"]
    ny = 1 << ((ns.bit_length() - 1) // 2)
    seq_head = P("seq", "head")
    return jax.shard_map(
        functools.partial(per_device, (ns // ny, ny), ns, nh),
        mesh=mesh,
        in_specs=(seq_head,) * 8 + (P("head"), P("head", None, None), seq_head),
        out_specs=(seq_head, seq_head, seq_head, P("head", None, None), P("head")),
        check_vma=False,
    )
```

```python
import functools
import math

import jax
import jax.numpy as jnp
from jax import lax
from jax.experimental import pallas as pl
from jax.experimental.pallas import tpu as pltpu
from jax.sharding import PartitionSpec as P

WINDOW = 128
LAGS = (4, 8, 12)
SHARES = 4
HEAD = 64
PAIR = 2 * HEAD
clip_scale = 64.0
limit_factor = 0.05
temper = 0.125
negative = -1e30
f32 = jnp.float32
bf16 = jnp.bfloat16
MESH = pl.DeviceIdType.MESH

NN = (((1,), (0,)), ((), ()))
NT = (((1,), (1,)), ((), ()))


def mm(a, b, dims=NN):
    return lax.dot_general(a, b, dims, preferred_element_type=f32)


def spread(ref, first, count, times, cols):
    width = WINDOW
    return jnp.concatenate(
        [jnp.broadcast_to(ref[first + r : first + r + 1, cols], (times, width)) for r in range(count)], axis=0
    )


def kernel(sizes, limit_value, *refs):
    (
        qe_hbm, qx_hbm, kt_hbm, kx_hbm, vt_hbm, vx_hbm, qc_hbm, kc_hbm, sinks, rot_hbm, do_hbm,
        gq_hbm, gk_hbm, gv_hbm, gr_hbm, gs_hbm,
        q_s, d_s, mq_s, qx_s, kt_s, kx_s, vt_s, vx_s, qc_s, kc_s, rot_s,
        scale_s, kv_t, k_row, v_row, dk_s, dv_s, d2_s, w_s, rb_s, part_s, sinkacc, tri_s, back_in, back_in_v, g_s, gk_s, gv_s, gr_s, gs_s,
        buf_a1, buf_b1, buf_a2, buf_b2, sq_buf,
        q_sem, d_sem, g_sem, in_sem, out_sem, halo_sem, back_sem,
        a1_send, a1_recv, b1_send, b1_recv, a2_send, a2_recv, b2_send, b2_recv, h_send, h_recv,
    ) = refs
    nz, ny, nh, blocks, heads = sizes
    ns = nz * ny
    pairs = heads // 2
    me_s = lax.axis_index("seq")
    me_h = lax.axis_index("head")
    me_z, me_y = me_s // ny, lax.rem(me_s, ny)
    nxt, prv = lax.rem(me_s + 1, ns), lax.rem(me_s + ns - 1, ns)

    def seq_dev(s):
        return (s, me_h)

    z_peers = [(lax.rem(me_z + k, nz)) for k in range(1, nz)]
    y_peers = [(lax.rem(me_y + k, ny)) for k in range(1, ny)]
    h_peers = [(lax.rem(me_h + k, nh)) for k in range(1, nh)]

    barrier = pltpu.get_barrier_semaphore()
    targets = [(nxt, me_h), (prv, me_h)]
    targets += [(z * ny + me_y, me_h) for z in z_peers]
    targets += [(me_z * ny + y, me_h) for y in y_peers]
    targets += [(me_s, h) for h in h_peers]
    for dev in targets:
        pl.semaphore_signal(barrier, inc=1, device_id=dev, device_id_type=MESH)

    small = [
        (kt_hbm, kt_s), (kx_hbm, kx_s), (vt_hbm, vt_s), (vx_hbm, vx_s),
        (qx_hbm, qx_s), (qc_hbm, qc_s), (kc_hbm, kc_s), (rot_hbm, rot_s),
    ]
    small_copies = [pltpu.make_async_copy(a, b, in_sem.at[n]) for n, (a, b) in enumerate(small)]
    for c in small_copies[:4]:
        c.start()

    def q_copy(b):
        rows = pl.ds(pl.multiple_of(b * WINDOW, WINDOW), WINDOW)
        return pltpu.make_async_copy(qe_hbm.at[rows], q_s.at[rows], q_sem.at[b])

    def d_copy(b):
        rows = pl.ds(pl.multiple_of(b * WINDOW, WINDOW), WINDOW)
        return pltpu.make_async_copy(do_hbm.at[rows], d_s.at[rows], d_sem.at[b])

    def g_copy(b):
        rows = pl.ds(pl.multiple_of(b * WINDOW, WINDOW), WINDOW)
        return pltpu.make_async_copy(g_s.at[rows], gq_hbm.at[rows], g_sem.at[b])

    for n in range(blocks):
        b = [1, 2, 3, 4, 0, 5, 6, 7][n]
        q_copy(b).start()
        d_copy(b).start()
        if n == 0:
            for c in small_copies[4:]:
                c.start()

    p_iota = lax.broadcasted_iota(jnp.int32, (WINDOW, 2 * WINDOW), 0)
    i_iota = lax.rem(lax.broadcasted_iota(jnp.int32, (WINDOW, 2 * WINDOW), 1), WINDOW)
    tri_s[...] = jnp.where(p_iota <= i_iota, 1.0, 0.0).astype(bf16)
    part_s[...] = jnp.zeros_like(part_s)
    sinkacc[...] = jnp.zeros_like(sinkacc)
    dk_s[...] = jnp.zeros_like(dk_s)
    dv_s[...] = jnp.zeros_like(dv_s)

    for c in small_copies[:4]:
        c.wait()
    ksc = jnp.exp2(kx_s[...].astype(f32)) * temper
    vsc = jnp.exp2(vx_s[...].astype(f32))
    for half in range(2):
        rr = slice(32 * half, 32 * half + 32)
        k8 = (kt_s[rr, :].astype(f32) * ksc[half : half + 1, :]).astype(bf16)
        vv = (vt_s[rr, :].astype(f32) * vsc[half : half + 1, :]).astype(bf16)
        kv_t[32 * half : 32 * half + 32, WINDOW:] = k8
        kv_t[HEAD + 32 * half : HEAD + 32 * half + 32, WINDOW:] = vv

    def rows_of(cb):
        at = pl.ds(pl.multiple_of(cb * WINDOW, WINDOW), WINDOW)
        both = kv_t[:, at]
        k_row[at, :] = both[:HEAD].T
        v_row[at, :] = both[HEAD:].T

    def rows_step(cb, carry):
        rows_of(cb)
        return carry

    lax.fori_loop(1, blocks + 1, rows_step, 0)

    for c in small_copies[4:]:
        c.wait()
    scale_s[...] = jnp.exp2(qx_s[...].astype(f32))
    rlow = rot_s[...].astype(bf16)
    rlow_t = rot_s[...].T.astype(bf16)
    zero = jnp.zeros((HEAD, HEAD), bf16)
    rb_s[...] = jnp.concatenate(
        [jnp.concatenate([rlow_t, zero], axis=1), jnp.concatenate([zero, rlow_t], axis=1)], axis=0
    )

    halo = pltpu.make_async_remote_copy(
        src_ref=kv_t.at[:, pl.ds(blocks * WINDOW, WINDOW)],
        dst_ref=kv_t.at[:, pl.ds(0, WINDOW)],
        send_sem=halo_sem.at[0], recv_sem=halo_sem.at[1],
        device_id=(nxt, me_h), device_id_type=MESH,
    )
    back = pltpu.make_async_remote_copy(
        src_ref=dk_s.at[:, pl.ds(0, WINDOW)],
        dst_ref=back_in,
        send_sem=back_sem.at[0], recv_sem=back_sem.at[1],
        device_id=(prv, me_h), device_id_type=MESH,
    )
    back_v = pltpu.make_async_remote_copy(
        src_ref=dv_s.at[:, pl.ds(0, WINDOW)],
        dst_ref=back_in_v,
        send_sem=back_sem.at[2], recv_sem=back_sem.at[3],
        device_id=(prv, me_h), device_id_type=MESH,
    )
    bits = jnp.left_shift(1, lax.broadcasted_iota(jnp.int32, (16, WINDOW), 0))
    bits64 = jnp.concatenate([bits] * 4, axis=0)

    sink_rows = [
        jnp.concatenate([jnp.full((1, WINDOW), sinks[2 * pr + h], f32) for h in range(2)], axis=1)
        for pr in range(pairs)
    ]

    def step(n, carry):
        @pl.when(n == 1)
        def _():
            pl.semaphore_wait(barrier, len(targets))
            halo.start()

        @pl.when(n == 2)
        def _():
            halo.wait()
            rows_of(0)

        both = [2 * n + 1 - jnp.where(n == 2, 5, 0) + jnp.where(n == 3, -1, 0), 2 * n + 2 - jnp.where(n >= 2, 1, 0)]
        views = []
        for b in both:
            q_copy(b).wait()
            d_copy(b).wait()
            cols = pl.ds(pl.multiple_of(b * WINDOW, WINDOW), WINDOW)
            wide = pl.ds(pl.multiple_of(b * WINDOW, WINDOW), 2 * WINDOW)
            views.append((b, cols, wide))
        hidden = jnp.where((both[0] == 0) & (me_s == 0), negative, 0.0)
        tri = p_iota <= i_iota
        trib = tri_s[...]
        units = [(k, pr) for k in range(2) for pr in range(pairs)]
        hold = {}

        def stage_a(k, pr):
            b, cols, wide = views[k]
            lanes = slice(pr * PAIR, (pr + 1) * PAIR)
            qt = q_s[cols, lanes].T * spread(scale_s, 4 * pr, 4, 32, cols).astype(bf16)
            dt = d_s[cols, lanes].T
            q2 = jnp.concatenate([qt[:HEAD], qt[HEAD:]], axis=1)
            d2 = jnp.concatenate([dt[:HEAD], dt[HEAD:]], axis=1)
            d2_s[b, :, 2 * pr * WINDOW : 2 * (pr + 1) * WINDOW] = d2
            s_all = mm(k_row[wide, :], q2)
            before = s_all[:WINDOW] + hidden if k == 0 else s_all[:WINDOW]
            s = jnp.where(tri, s_all[WINDOW:], before)
            dp_all = mm(v_row[wide, :], d2)
            dp = jnp.where(tri, dp_all[WINDOW:], dp_all[:WINDOW])
            hold[k, pr] = (q2, s, dp)

        def stage_b(k, pr):
            b, cols, wide = views[k]
            q2, s, dp = hold[k, pr]
            sink = sink_rows[pr]
            top = jnp.maximum(jnp.max(s, axis=0, keepdims=True), sink)
            e = jnp.exp(s - top)
            es = jnp.exp(sink - top)
            inv = 1.0 / (jnp.sum(e, axis=0, keepdims=True) + es)
            w = e * inv
            t = w * dp
            delta = jnp.sum(t, axis=0, keepdims=True)
            ds = t - w * delta
            sk = es * inv * delta
            sinkacc[2 * pr : 2 * pr + 1, :] -= sk[:, :WINDOW]
            sinkacc[2 * pr + 1 : 2 * pr + 2, :] -= sk[:, WINDOW:]
            w_s[b, :, 2 * pr * WINDOW : 2 * (pr + 1) * WINDOW] = w.astype(bf16)
            sb = ds.astype(bf16)
            s_cur = sb * trib
            hold[k, pr] = (q2, jnp.concatenate([sb - s_cur, s_cur], axis=0))

        def stage_c(k, pr):
            b, cols, wide = views[k]
            q2, s2 = hold[k, pr]
            gqt = mm(kv_t[:HEAD, wide], s2)
            dk = mm(q2, s2, NT)
            dks[k] = dk if dks[k] is None else dks[k] + dk
            hold[k, pr] = (q2, gqt)

        def stage_d(k, pr):
            b, cols, wide = views[k]
            lanes = slice(pr * PAIR, (pr + 1) * PAIR)
            q2, gqt = hold.pop((k, pr))
            m2 = []
            for h in range(2):
                words = spread(qc_s, 4 * (2 * pr + h), 4, 16, cols)
                keep = jnp.bitwise_and(words, bits64) != 0
                m2.append(jnp.where(keep, gqt[:, h * WINDOW : (h + 1) * WINDOW], 0.0).astype(bf16))
            mq_s[lanes, cols] = jnp.concatenate(m2, axis=0)
            part = mm(q2, jnp.concatenate(m2, axis=1), NT)
            parts[0] = part if parts[0] is None else parts[0] + part

        dks = [None, None]
        parts = [None]
        for t in range(len(units) + LAGS[2]):
            for lag, stage in zip((0,) + LAGS, (stage_a, stage_b, stage_c, stage_d)):
                if 0 <= t - lag < len(units):
                    stage(*units[t - lag])
        for (b, cols, wide), dk in zip(views, dks):
            dk_s[:, wide] += dk
        part_s[...] += parts[0]

        @pl.when(n == 2)
        def _():
            back.start()

        return carry

    lax.fori_loop(0, blocks // 2, step, 0)
    back.wait()

    last = pl.ds(blocks * WINDOW, WINDOW)
    dk_s[:, last] += back_in[...]

    keep = jnp.bitwise_and(
        jnp.concatenate([jnp.broadcast_to(kc_s[r : r + 1, :], (16, blocks * WINDOW)) for r in range(4)], axis=0),
        jnp.left_shift(1, lax.rem(lax.broadcasted_iota(jnp.int32, (HEAD, blocks * WINDOW), 0), 16)),
    ) != 0
    mk = jnp.where(keep, dk_s[:, WINDOW:] * temper, 0.0).astype(bf16)
    gk_s[...] = mk
    part_s[...] += mm(kv_t[:HEAD, WINDOW:], mk, NT) * (1.0 / temper)

    cut = buf_a1.shape[1]
    part = part_s[...]
    folded = jnp.concatenate([part[: HEAD // 2], part[HEAD // 2 :]], axis=1)
    buf_a1[pl.ds(me_z, 1)] = folded[:cut].astype(bf16)[None]
    buf_b1[pl.ds(me_y, 1)] = (
        jnp.concatenate([folded[cut:], sinkacc[...], jnp.zeros_like(sinkacc)], axis=0).astype(bf16)[None]
    )

    def exchange(buf, me, peers, device, send, recv):
        copies = []
        for k, peer in enumerate(peers):
            copies.append(
                pltpu.make_async_remote_copy(
                    src_ref=buf.at[me], dst_ref=buf.at[me],
                    send_sem=send.at[k], recv_sem=recv.at[k],
                    device_id=device(peer), device_id_type=MESH,
                )
            )
        for c in copies:
            c.start()
        return copies

    def along_z(z):
        return (z * ny + me_y, me_h)

    def along_y(y):
        return (me_z * ny + y, me_h)

    def along_h(h):
        return (me_s, h)

    def total(buf, count):
        acc = buf[0].astype(f32)
        for k in range(1, count):
            acc = acc + buf[k].astype(f32)
        return acc

    copies_a = exchange(buf_a1, me_z, z_peers, along_z, a1_send, a1_recv)
    copies_b = exchange(buf_b1, me_y, y_peers, along_y, b1_send, b1_recv)

    def turn(b, carry):
        cols = pl.ds(pl.multiple_of(b * WINDOW, WINDOW), WINDOW)
        for pr in range(pairs):
            lanes = slice(pr * PAIR, (pr + 1) * PAIR)
            g_s[cols, lanes] = mm(mq_s[lanes, cols].T, rb_s[...]).astype(bf16)
        g_copy(b).start()
        return carry

    def values(b, carry):
        wide = pl.ds(pl.multiple_of(b * WINDOW, WINDOW), 2 * WINDOW)
        wb = w_s[b]
        w_cur = wb * jnp.concatenate([tri_s[...]] * pairs, axis=1)
        dv_s[:, wide] += mm(d2_s[b], jnp.concatenate([wb - w_cur, w_cur], axis=0), NT)
        return carry

    values(0, 0)
    back_v.start()
    lax.fori_loop(1, blocks, values, 0)
    for c in copies_a:
        c.wait()
    buf_a2[pl.ds(me_y, 1)] = total(buf_a1, nz).astype(bf16)[None]
    copies_a = exchange(buf_a2, me_y, y_peers, along_y, a2_send, a2_recv)
    for c in copies_b:
        c.wait()
    buf_b2[pl.ds(me_z, 1)] = total(buf_b1, ny).astype(bf16)[None]
    copies_b = exchange(buf_b2, me_z, z_peers, along_z, b2_send, b2_recv)
    lax.fori_loop(0, blocks, turn, 0)
    for c in copies_a:
        c.wait()
    for c in copies_b:
        c.wait()
    tot_a = total(buf_a2, ny)
    tot_b = total(buf_b2, nz)
    rows_b = HEAD // 2 - cut
    whole = jnp.concatenate([tot_a, tot_b[:rows_b]], axis=0)
    summed = jnp.concatenate([whole[:, :HEAD], whole[:, HEAD:]], axis=0)
    raw = lax.dot_general(
        rot_s[...], summed, NN, precision=lax.Precision.HIGHEST, preferred_element_type=f32
    )
    sq = jnp.sum(jnp.sum(raw * raw, axis=0, keepdims=True), axis=1, keepdims=True)
    sq_buf[pl.ds(me_h, 1)] = jnp.broadcast_to(sq, (8, 128))[None]
    copies_h = exchange(sq_buf, me_h, h_peers, along_h, h_send, h_recv)
    gs_s[...] = jnp.sum(tot_b[rows_b : rows_b + heads].T, axis=0, keepdims=True)
    gk_s[...] = mm(rlow, gk_s[...]).astype(bf16)
    back_v.wait()
    dv_s[:, last] += back_in_v[...]
    gv_s[...] = dv_s[:, WINDOW:].astype(bf16)
    outs = [
        pltpu.make_async_copy(a, b, out_sem.at[n])
        for n, (a, b) in enumerate([(gk_s, gk_hbm), (gv_s, gv_hbm), (gs_s, gs_hbm), (gr_s, gr_hbm)])
    ]
    for c in outs[:3]:
        c.start()
    for c in copies_h:
        c.wait()
    norm = jnp.sqrt(total(sq_buf, nh)[:1, :HEAD])
    gr_s[...] = raw * (clip_scale / jnp.maximum(norm, limit_value))
    outs[3].start()

    def g_wait(b, carry):
        g_copy(b).wait()
        return carry

    lax.fori_loop(0, blocks, g_wait, 0)
    for c in outs:
        c.wait()


def store(*refs):
    srcs, dsts, held, in_sems, out_sems = refs[:5], refs[5:10], refs[10:15], refs[15], refs[16]
    parts = [(n, None) for n in (4, 3)]
    share = srcs[0].shape[0] // SHARES
    parts += [(0, pl.ds(n * share, share)) for n in range(SHARES)]
    parts += [(n, None) for n in (1, 2)]

    def view(ref, rows):
        return ref if rows is None else ref.at[rows]

    loads = [
        pltpu.make_async_copy(view(srcs[n], rows), view(held[n], rows), in_sems.at[k])
        for k, (n, rows) in enumerate(parts)
    ]
    stores = [
        pltpu.make_async_copy(view(held[n], rows), view(dsts[n], rows), out_sems.at[k])
        for k, (n, rows) in enumerate(parts)
    ]
    for c in loads:
        c.start()
    for c, d in zip(loads, stores):
        c.wait()
        d.start()
    for d in stores:
        d.wait()


def per_device(split, ns, nh, qe, qx, ke, kx, ve, vx, qc, kc, sinks, rot, dout):
    tokens, width = qe.shape
    heads = width // HEAD
    blocks = tokens // WINDOW
    nz, ny = split
    limit_value = limit_factor * math.sqrt(tokens * ns * heads * nh * HEAD)
    cut = 16
    rest = HEAD // 2 - cut + 16
    any_space = pl.BlockSpec(memory_space=pl.ANY)
    vmem = pltpu.VMEM
    dma = pltpu.SemaphoreType.DMA
    ext = tokens + WINDOW
    shapes = (
        jax.ShapeDtypeStruct((tokens, width), bf16),
        jax.ShapeDtypeStruct((HEAD, tokens), bf16),
        jax.ShapeDtypeStruct((HEAD, tokens), bf16),
        jax.ShapeDtypeStruct((HEAD, HEAD), f32),
        jax.ShapeDtypeStruct((1, heads), f32),
    )
    outs = pl.pallas_call(
        functools.partial(kernel, (nz, ny, nh, blocks, heads), limit_value),
        out_shape=shapes,
        in_specs=[any_space] * 8 + [pl.BlockSpec(memory_space=pltpu.SMEM)] + [any_space] * 2,
        out_specs=(any_space,) * 5,
        scratch_shapes=[
            vmem((tokens, width), bf16),
            vmem((tokens, width), bf16),
            vmem((width, tokens), bf16),
            vmem((2 * heads, tokens), jnp.int32),
            vmem((HEAD, tokens), bf16),
            vmem((2, tokens), jnp.int32),
            vmem((HEAD, tokens), bf16),
            vmem((2, tokens), jnp.int32),
            vmem((4 * heads, tokens), jnp.int32),
            vmem((4, tokens), jnp.int32),
            vmem((HEAD, HEAD), f32),
            vmem((2 * heads, tokens), f32),
            vmem((2 * HEAD, ext), bf16),
            vmem((ext, HEAD), bf16),
            vmem((ext, HEAD), bf16),
            vmem((HEAD, ext), f32),
            vmem((HEAD, ext), f32),
            vmem((blocks, HEAD, heads * WINDOW), bf16),
            vmem((blocks, WINDOW, heads * WINDOW), bf16),
            vmem((PAIR, PAIR), bf16),
            vmem((HEAD, HEAD), f32),
            vmem((heads, WINDOW), f32),
            vmem((WINDOW, 2 * WINDOW), bf16),
            vmem((HEAD, WINDOW), f32),
            vmem((HEAD, WINDOW), f32),
            vmem((tokens, width), bf16),
            vmem((HEAD, tokens), bf16),
            vmem((HEAD, tokens), bf16),
            vmem((HEAD, HEAD), f32),
            vmem((1, heads), f32),
            vmem((nz, cut, 128), bf16),
            vmem((ny, rest, 128), bf16),
            vmem((ny, cut, 128), bf16),
            vmem((nz, rest, 128), bf16),
            vmem((nh, 8, 128), f32),
            dma((blocks,)),
            dma((blocks,)),
            dma((blocks,)),
            dma((8,)),
            dma((4,)),
            dma((2,)),
            dma((4,)),
            dma((nz,)), dma((nz,)), dma((ny,)), dma((ny,)),
            dma((ny,)), dma((ny,)), dma((nz,)), dma((nz,)),
            dma((nh,)), dma((nh,)),
        ],
        compiler_params=pltpu.CompilerParams(
            collective_id=0, has_side_effects=True, vmem_limit_bytes=61 * 1024 * 1024
        ),
    )(qe, qx.T, ke.T, kx.T, ve.T, vx.T, qc.T, kc.T, sinks, rot.reshape(HEAD, HEAD), dout)
    gq, gk, gv, gr, gs = pl.pallas_call(
        store,
        out_shape=shapes,
        in_specs=[any_space] * 5,
        out_specs=(any_space,) * 5,
        scratch_shapes=[vmem(x.shape, x.dtype) for x in shapes] + [dma((SHARES + 4,))] * 2,
    )(*outs)
    return (gq, gk.T, gv.T, gr[None], gs.reshape(heads))


def solution(mesh):
    ns, nh = mesh.shape["seq"], mesh.shape["head"]
    ny = 1 << ((ns.bit_length() - 1) // 2)
    seq_head = P("seq", "head")
    return jax.shard_map(
        functools.partial(per_device, (ns // ny, ny), ns, nh),
        mesh=mesh,
        in_specs=(seq_head,) * 8 + (P("head"), P("head", None, None), seq_head),
        out_specs=(seq_head, seq_head, seq_head, P("head", None, None), P("head")),
        check_vma=False,
    )
```

```python
import functools
import math

import jax
import jax.numpy as jnp
from jax import lax
from jax.experimental import pallas as pl
from jax.experimental.pallas import tpu as pltpu
from jax.sharding import PartitionSpec as P

WINDOW = 128
LAGS = (4, 8, 12)
SHARES = 1
HEAD = 64
PAIR = 2 * HEAD
clip_scale = 64.0
limit_factor = 0.05
temper = 0.125
negative = -1e30
f32 = jnp.float32
bf16 = jnp.bfloat16
MESH = pl.DeviceIdType.MESH

NN = (((1,), (0,)), ((), ()))
NT = (((1,), (1,)), ((), ()))


def mm(a, b, dims=NN):
    return lax.dot_general(a, b, dims, preferred_element_type=f32)


def spread(ref, first, count, times, cols):
    width = WINDOW
    return jnp.concatenate(
        [jnp.broadcast_to(ref[first + r : first + r + 1, cols], (times, width)) for r in range(count)], axis=0
    )


def kernel(sizes, limit_value, *refs):
    (
        qe_hbm, qx_hbm, kt_hbm, kx_hbm, vt_hbm, vx_hbm, qc_hbm, kc_hbm, sinks, rot_hbm, do_hbm,
        g_s, gk_s, gv_s, gr_s, gs_s,
        q_s, d_s, mq_s, qx_s, kt_s, kx_s, vt_s, vx_s, qc_s, kc_s, rot_s,
        scale_s, kv_t, k_row, v_row, dk_s, dv_s, d2_s, w_s, rb_s, part_s, sinkacc, tri_s, back_in, back_in_v,
        buf_a1, buf_b1, buf_a2, buf_b2, sq_buf,
        q_sem, d_sem, in_sem, halo_sem, back_sem,
        a1_send, a1_recv, b1_send, b1_recv, a2_send, a2_recv, b2_send, b2_recv, h_send, h_recv,
    ) = refs
    nz, ny, nh, blocks, heads = sizes
    ns = nz * ny
    pairs = heads // 2
    me_s = lax.axis_index("seq")
    me_h = lax.axis_index("head")
    me_z, me_y = me_s // ny, lax.rem(me_s, ny)
    nxt, prv = lax.rem(me_s + 1, ns), lax.rem(me_s + ns - 1, ns)

    def seq_dev(s):
        return (s, me_h)

    z_peers = [(lax.rem(me_z + k, nz)) for k in range(1, nz)]
    y_peers = [(lax.rem(me_y + k, ny)) for k in range(1, ny)]
    h_peers = [(lax.rem(me_h + k, nh)) for k in range(1, nh)]

    barrier = pltpu.get_barrier_semaphore()
    targets = [(nxt, me_h), (prv, me_h)]
    targets += [(z * ny + me_y, me_h) for z in z_peers]
    targets += [(me_z * ny + y, me_h) for y in y_peers]
    targets += [(me_s, h) for h in h_peers]
    for dev in targets:
        pl.semaphore_signal(barrier, inc=1, device_id=dev, device_id_type=MESH)

    small = [
        (kt_hbm, kt_s), (kx_hbm, kx_s), (vt_hbm, vt_s), (vx_hbm, vx_s),
        (qx_hbm, qx_s), (qc_hbm, qc_s), (kc_hbm, kc_s), (rot_hbm, rot_s),
    ]
    small_copies = [pltpu.make_async_copy(a, b, in_sem.at[n]) for n, (a, b) in enumerate(small)]
    for c in small_copies[:4]:
        c.start()

    def q_copy(b):
        rows = pl.ds(pl.multiple_of(b * WINDOW, WINDOW), WINDOW)
        return pltpu.make_async_copy(qe_hbm.at[rows], q_s.at[rows], q_sem.at[b])

    def d_copy(b):
        rows = pl.ds(pl.multiple_of(b * WINDOW, WINDOW), WINDOW)
        return pltpu.make_async_copy(do_hbm.at[rows], d_s.at[rows], d_sem.at[b])

    for n in range(blocks):
        b = [1, 2, 3, 4, 0, 5, 6, 7][n]
        q_copy(b).start()
        d_copy(b).start()
        if n == 0:
            for c in small_copies[4:]:
                c.start()

    p_iota = lax.broadcasted_iota(jnp.int32, (WINDOW, 2 * WINDOW), 0)
    i_iota = lax.rem(lax.broadcasted_iota(jnp.int32, (WINDOW, 2 * WINDOW), 1), WINDOW)
    tri_s[...] = jnp.where(p_iota <= i_iota, 1.0, 0.0).astype(bf16)
    part_s[...] = jnp.zeros_like(part_s)
    sinkacc[...] = jnp.zeros_like(sinkacc)
    dk_s[...] = jnp.zeros_like(dk_s)
    dv_s[...] = jnp.zeros_like(dv_s)

    for c in small_copies[:4]:
        c.wait()
    ksc = jnp.exp2(kx_s[...].astype(f32)) * temper
    vsc = jnp.exp2(vx_s[...].astype(f32))
    for half in range(2):
        rr = slice(32 * half, 32 * half + 32)
        k8 = (kt_s[rr, :].astype(f32) * ksc[half : half + 1, :]).astype(bf16)
        vv = (vt_s[rr, :].astype(f32) * vsc[half : half + 1, :]).astype(bf16)
        kv_t[32 * half : 32 * half + 32, WINDOW:] = k8
        kv_t[HEAD + 32 * half : HEAD + 32 * half + 32, WINDOW:] = vv

    def rows_of(cb):
        at = pl.ds(pl.multiple_of(cb * WINDOW, WINDOW), WINDOW)
        both = kv_t[:, at]
        k_row[at, :] = both[:HEAD].T
        v_row[at, :] = both[HEAD:].T

    def rows_step(cb, carry):
        rows_of(cb)
        return carry

    lax.fori_loop(1, blocks + 1, rows_step, 0, unroll=True)

    for c in small_copies[4:]:
        c.wait()
    scale_s[...] = jnp.exp2(qx_s[...].astype(f32))
    rlow = rot_s[...].astype(bf16)
    rlow_t = rot_s[...].T.astype(bf16)
    zero = jnp.zeros((HEAD, HEAD), bf16)
    rb_s[...] = jnp.concatenate(
        [jnp.concatenate([rlow_t, zero], axis=1), jnp.concatenate([zero, rlow_t], axis=1)], axis=0
    )

    halo = pltpu.make_async_remote_copy(
        src_ref=kv_t.at[:, pl.ds(blocks * WINDOW, WINDOW)],
        dst_ref=kv_t.at[:, pl.ds(0, WINDOW)],
        send_sem=halo_sem.at[0], recv_sem=halo_sem.at[1],
        device_id=(nxt, me_h), device_id_type=MESH,
    )
    back = pltpu.make_async_remote_copy(
        src_ref=dk_s.at[:, pl.ds(0, WINDOW)],
        dst_ref=back_in,
        send_sem=back_sem.at[0], recv_sem=back_sem.at[1],
        device_id=(prv, me_h), device_id_type=MESH,
    )
    back_v = pltpu.make_async_remote_copy(
        src_ref=dv_s.at[:, pl.ds(0, WINDOW)],
        dst_ref=back_in_v,
        send_sem=back_sem.at[2], recv_sem=back_sem.at[3],
        device_id=(prv, me_h), device_id_type=MESH,
    )
    bits = jnp.left_shift(1, lax.broadcasted_iota(jnp.int32, (16, WINDOW), 0))
    bits64 = jnp.concatenate([bits] * 4, axis=0)

    sink_rows = [
        jnp.concatenate([jnp.full((1, WINDOW), sinks[2 * pr + h], f32) for h in range(2)], axis=1)
        for pr in range(pairs)
    ]

    ahead = lax.rem(lax.broadcasted_iota(jnp.int32, (8, 2 * WINDOW), 1), WINDOW) - lax.broadcasted_iota(
        jnp.int32, (8, 2 * WINDOW), 0
    )

    def step(n, carry):
        @pl.when(n == 1)
        def _():
            pl.semaphore_wait(barrier, len(targets))
            halo.start()

        @pl.when(n == 2)
        def _():
            halo.wait()
            rows_of(0)

        both = [2 * n + 1 - jnp.where(n == 2, 5, 0) + jnp.where(n == 3, -1, 0), 2 * n + 2 - jnp.where(n >= 2, 1, 0)]
        views = []
        for b in both:
            q_copy(b).wait()
            d_copy(b).wait()
            cols = pl.ds(pl.multiple_of(b * WINDOW, WINDOW), WINDOW)
            wide = pl.ds(pl.multiple_of(b * WINDOW, WINDOW), 2 * WINDOW)
            views.append((b, cols, wide))
        hidden = jnp.where((both[0] == 0) & (me_s == 0), negative, 0.0)
        trib = tri_s[...]
        units = [(k, pr) for k in range(2) for pr in range(pairs)]
        hold = {}

        def choose(now, past):
            return jnp.concatenate(
                [jnp.where(ahead >= r, now[r : r + 8], past[r : r + 8]) for r in range(0, WINDOW, 8)], axis=0
            )

        def stage_a(k, pr):
            b, cols, wide = views[k]
            lanes = slice(pr * PAIR, (pr + 1) * PAIR)
            qt = q_s[cols, lanes].T * spread(scale_s, 4 * pr, 4, 32, cols).astype(bf16)
            dt = d_s[cols, lanes].T
            q2 = jnp.concatenate([qt[:HEAD], qt[HEAD:]], axis=1)
            d2 = jnp.concatenate([dt[:HEAD], dt[HEAD:]], axis=1)
            d2_s[b, :, 2 * pr * WINDOW : 2 * (pr + 1) * WINDOW] = d2
            s_all = mm(k_row[wide, :], q2)
            before = s_all[:WINDOW] + hidden if k == 0 else s_all[:WINDOW]
            s = choose(s_all[WINDOW:], before)
            dp_all = mm(v_row[wide, :], d2)
            dp = choose(dp_all[WINDOW:], dp_all[:WINDOW])
            hold[k, pr] = (q2, s, dp)

        def stage_b(k, pr):
            b, cols, wide = views[k]
            q2, s, dp = hold[k, pr]
            sink = sink_rows[pr]
            top = jnp.maximum(jnp.max(s, axis=0, keepdims=True), sink)
            e = jnp.exp(s - top)
            es = jnp.exp(sink - top)
            inv = 1.0 / (jnp.sum(e, axis=0, keepdims=True) + es)
            w = e * inv
            t = w * dp
            delta = jnp.sum(t, axis=0, keepdims=True)
            ds = t - w * delta
            sk = es * inv * delta
            sinkacc[2 * pr : 2 * pr + 1, :] -= sk[:, :WINDOW]
            sinkacc[2 * pr + 1 : 2 * pr + 2, :] -= sk[:, WINDOW:]
            w_s[b, :, 2 * pr * WINDOW : 2 * (pr + 1) * WINDOW] = w.astype(bf16)
            sb = ds.astype(bf16)
            s_cur = sb * trib
            hold[k, pr] = (q2, jnp.concatenate([sb - s_cur, s_cur], axis=0))

        def stage_c(k, pr):
            b, cols, wide = views[k]
            q2, s2 = hold[k, pr]
            gqt = mm(kv_t[:HEAD, wide], s2)
            dk = mm(q2, s2, NT)
            dks[k] = dk if dks[k] is None else dks[k] + dk
            hold[k, pr] = (q2, gqt)

        def stage_d(k, pr):
            b, cols, wide = views[k]
            lanes = slice(pr * PAIR, (pr + 1) * PAIR)
            q2, gqt = hold.pop((k, pr))
            m2 = []
            for h in range(2):
                words = spread(qc_s, 4 * (2 * pr + h), 4, 16, cols)
                keep = jnp.bitwise_and(words, bits64) != 0
                m2.append(jnp.where(keep, gqt[:, h * WINDOW : (h + 1) * WINDOW], 0.0).astype(bf16))
            mq_s[lanes, cols] = jnp.concatenate(m2, axis=0)
            part = mm(q2, jnp.concatenate(m2, axis=1), NT)
            parts[0] = part if parts[0] is None else parts[0] + part

        dks = [None, None]
        parts = [None]
        for t in range(len(units) + LAGS[2]):
            for lag, stage in zip((0,) + LAGS, (stage_a, stage_b, stage_c, stage_d)):
                if 0 <= t - lag < len(units):
                    stage(*units[t - lag])
        for (b, cols, wide), dk in zip(views, dks):
            dk_s[:, wide] += dk
        part_s[...] += parts[0]

        @pl.when(n == 2)
        def _():
            back.start()

        return carry

    lax.fori_loop(0, blocks // 2, step, 0)
    back.wait()

    last = pl.ds(blocks * WINDOW, WINDOW)
    dk_s[:, last] += back_in[...]

    keep = jnp.bitwise_and(
        jnp.concatenate([jnp.broadcast_to(kc_s[r : r + 1, :], (16, blocks * WINDOW)) for r in range(4)], axis=0),
        jnp.left_shift(1, lax.rem(lax.broadcasted_iota(jnp.int32, (HEAD, blocks * WINDOW), 0), 16)),
    ) != 0
    mk = jnp.where(keep, dk_s[:, WINDOW:] * temper, 0.0).astype(bf16)
    gk_s[...] = mk
    part_s[...] += mm(kv_t[:HEAD, WINDOW:], mk, NT) * (1.0 / temper)

    cut = buf_a1.shape[1]
    part = part_s[...]
    folded = jnp.concatenate([part[: HEAD // 2], part[HEAD // 2 :]], axis=1)
    buf_a1[pl.ds(me_z, 1)] = folded[:cut].astype(bf16)[None]
    buf_b1[pl.ds(me_y, 1)] = (
        jnp.concatenate([folded[cut:], sinkacc[...], jnp.zeros_like(sinkacc)], axis=0).astype(bf16)[None]
    )

    def exchange(buf, me, peers, device, send, recv):
        copies = []
        for k, peer in enumerate(peers):
            copies.append(
                pltpu.make_async_remote_copy(
                    src_ref=buf.at[me], dst_ref=buf.at[me],
                    send_sem=send.at[k], recv_sem=recv.at[k],
                    device_id=device(peer), device_id_type=MESH,
                )
            )
        for c in copies:
            c.start()
        return copies

    def along_z(z):
        return (z * ny + me_y, me_h)

    def along_y(y):
        return (me_z * ny + y, me_h)

    def along_h(h):
        return (me_s, h)

    def total(buf, count):
        acc = buf[0].astype(f32)
        for k in range(1, count):
            acc = acc + buf[k].astype(f32)
        return acc

    copies_a = exchange(buf_a1, me_z, z_peers, along_z, a1_send, a1_recv)
    copies_b = exchange(buf_b1, me_y, y_peers, along_y, b1_send, b1_recv)

    def turn(b, carry):
        cols = pl.ds(pl.multiple_of(b * WINDOW, WINDOW), WINDOW)
        for pr in range(pairs):
            lanes = slice(pr * PAIR, (pr + 1) * PAIR)
            g_s[cols, lanes] = mm(mq_s[lanes, cols].T, rb_s[...]).astype(bf16)
        return carry

    def values(b, carry):
        wide = pl.ds(pl.multiple_of(b * WINDOW, WINDOW), 2 * WINDOW)
        wb = w_s[b]
        w_cur = wb * jnp.concatenate([tri_s[...]] * pairs, axis=1)
        dv_s[:, wide] += mm(d2_s[b], jnp.concatenate([wb - w_cur, w_cur], axis=0), NT)
        return carry

    values(0, 0)
    back_v.start()
    lax.fori_loop(1, blocks, values, 0)
    for c in copies_a:
        c.wait()
    buf_a2[pl.ds(me_y, 1)] = total(buf_a1, nz).astype(bf16)[None]
    copies_a = exchange(buf_a2, me_y, y_peers, along_y, a2_send, a2_recv)
    for c in copies_b:
        c.wait()
    buf_b2[pl.ds(me_z, 1)] = total(buf_b1, ny).astype(bf16)[None]
    copies_b = exchange(buf_b2, me_z, z_peers, along_z, b2_send, b2_recv)
    lax.fori_loop(0, blocks, turn, 0)
    for c in copies_a:
        c.wait()
    for c in copies_b:
        c.wait()
    tot_a = total(buf_a2, ny)
    tot_b = total(buf_b2, nz)
    rows_b = HEAD // 2 - cut
    whole = jnp.concatenate([tot_a, tot_b[:rows_b]], axis=0)
    summed = jnp.concatenate([whole[:, :HEAD], whole[:, HEAD:]], axis=0)
    raw = lax.dot_general(
        rot_s[...], summed, NN, precision=lax.Precision.HIGHEST, preferred_element_type=f32
    )
    sq = jnp.sum(jnp.sum(raw * raw, axis=0, keepdims=True), axis=1, keepdims=True)
    sq_buf[pl.ds(me_h, 1)] = jnp.broadcast_to(sq, (8, 128))[None]
    copies_h = exchange(sq_buf, me_h, h_peers, along_h, h_send, h_recv)
    gs_s[...] = jnp.sum(tot_b[rows_b : rows_b + heads].T, axis=0, keepdims=True)
    gk_s[...] = mm(rlow, gk_s[...]).astype(bf16)
    back_v.wait()
    dv_s[:, last] += back_in_v[...]
    gv_s[...] = dv_s[:, WINDOW:].astype(bf16)
    for c in copies_h:
        c.wait()
    norm = jnp.sqrt(total(sq_buf, nh)[:1, :HEAD])
    gr_s[...] = raw * (clip_scale / jnp.maximum(norm, limit_value))


def store(*refs):
    srcs, dsts, sems = refs[:5], refs[5:10], refs[10]
    share = srcs[0].shape[0] // SHARES
    parts = [(n, None) for n in (4, 3, 2, 1)] + [(0, pl.ds(n * share, share)) for n in range(SHARES)]

    def view(ref, rows):
        return ref if rows is None else ref.at[rows]

    copies = [
        pltpu.make_async_copy(view(srcs[n], rows), view(dsts[n], rows), sems.at[k])
        for k, (n, rows) in enumerate(parts)
    ]
    for c in copies:
        c.start()
    for c in copies:
        c.wait()


def per_device(split, ns, nh, qe, qx, ke, kx, ve, vx, qc, kc, sinks, rot, dout):
    tokens, width = qe.shape
    heads = width // HEAD
    blocks = tokens // WINDOW
    nz, ny = split
    limit_value = limit_factor * math.sqrt(tokens * ns * heads * nh * HEAD)
    cut = 16
    rest = HEAD // 2 - cut + 16
    any_space = pl.BlockSpec(memory_space=pl.ANY)
    vmem = pltpu.VMEM
    dma = pltpu.SemaphoreType.DMA
    ext = tokens + WINDOW
    shapes = (
        jax.ShapeDtypeStruct((tokens, width), bf16),
        jax.ShapeDtypeStruct((HEAD, tokens), bf16),
        jax.ShapeDtypeStruct((HEAD, tokens), bf16),
        jax.ShapeDtypeStruct((HEAD, HEAD), f32),
        jax.ShapeDtypeStruct((1, heads), f32),
    )
    outs = pl.pallas_call(
        functools.partial(kernel, (nz, ny, nh, blocks, heads), limit_value),
        out_shape=shapes,
        in_specs=[any_space] * 8 + [pl.BlockSpec(memory_space=pltpu.SMEM)] + [any_space] * 2,
        out_specs=(pl.BlockSpec(memory_space=pltpu.VMEM),) * 5,
        scratch_shapes=[
            vmem((tokens, width), bf16),
            vmem((tokens, width), bf16),
            vmem((width, tokens), bf16),
            vmem((2 * heads, tokens), jnp.int32),
            vmem((HEAD, tokens), bf16),
            vmem((2, tokens), jnp.int32),
            vmem((HEAD, tokens), bf16),
            vmem((2, tokens), jnp.int32),
            vmem((4 * heads, tokens), jnp.int32),
            vmem((4, tokens), jnp.int32),
            vmem((HEAD, HEAD), f32),
            vmem((2 * heads, tokens), f32),
            vmem((2 * HEAD, ext), bf16),
            vmem((ext, HEAD), bf16),
            vmem((ext, HEAD), bf16),
            vmem((HEAD, ext), f32),
            vmem((HEAD, ext), f32),
            vmem((blocks, HEAD, heads * WINDOW), bf16),
            vmem((blocks, WINDOW, heads * WINDOW), bf16),
            vmem((PAIR, PAIR), bf16),
            vmem((HEAD, HEAD), f32),
            vmem((heads, WINDOW), f32),
            vmem((WINDOW, 2 * WINDOW), bf16),
            vmem((HEAD, WINDOW), f32),
            vmem((HEAD, WINDOW), f32),
            vmem((nz, cut, 128), bf16),
            vmem((ny, rest, 128), bf16),
            vmem((ny, cut, 128), bf16),
            vmem((nz, rest, 128), bf16),
            vmem((nh, 8, 128), f32),
            dma((blocks,)),
            dma((blocks,)),
            dma((8,)),
            dma((2,)),
            dma((4,)),
            dma((nz,)), dma((nz,)), dma((ny,)), dma((ny,)),
            dma((ny,)), dma((ny,)), dma((nz,)), dma((nz,)),
            dma((nh,)), dma((nh,)),
        ],
        compiler_params=pltpu.CompilerParams(
            collective_id=0, has_side_effects=True, vmem_limit_bytes=52 * 1024 * 1024
        ),
    )(*[pltpu.with_memory_space_constraint(x, pltpu.HBM) for x in (qe, qx.T, ke.T, kx.T, ve.T, vx.T, qc.T, kc.T, sinks, rot.reshape(HEAD, HEAD), dout)])
    gq, gk, gv, gr, gs = pl.pallas_call(
        store,
        out_shape=shapes,
        in_specs=[any_space] * 5,
        out_specs=(any_space,) * 5,
        scratch_shapes=[dma((SHARES + 4,))],
        compiler_params=pltpu.CompilerParams(vmem_limit_bytes=4 * 1024 * 1024),
    )(*outs)
    return (gq, gk.T, gv.T, gr[None], gs.reshape(heads))


def solution(mesh):
    ns, nh = mesh.shape["seq"], mesh.shape["head"]
    ny = 1 << ((ns.bit_length() - 1) // 2)
    seq_head = P("seq", "head")
    return jax.shard_map(
        functools.partial(per_device, (ns // ny, ny), ns, nh),
        mesh=mesh,
        in_specs=(seq_head,) * 8 + (P("head"), P("head", None, None), seq_head),
        out_specs=(seq_head, seq_head, seq_head, P("head", None, None), P("head")),
        check_vma=False,
    )
```

```python
import functools
import math

import jax
import jax.numpy as jnp
from jax import lax
from jax.experimental import pallas as pl
from jax.experimental.pallas import tpu as pltpu
from jax.sharding import PartitionSpec as P

WINDOW = 128
LAGS = (4, 8, 12)
SHARES = 1
HEAD = 64
PAIR = 2 * HEAD
clip_scale = 64.0
limit_factor = 0.05
temper = 0.125
negative = -1e30
f32 = jnp.float32
bf16 = jnp.bfloat16
MESH = pl.DeviceIdType.MESH

NN = (((1,), (0,)), ((), ()))
NT = (((1,), (1,)), ((), ()))


def mm(a, b, dims=NN):
    return lax.dot_general(a, b, dims, preferred_element_type=f32)


def spread(ref, first, count, times, cols):
    width = WINDOW
    return jnp.concatenate(
        [jnp.broadcast_to(ref[first + r : first + r + 1, cols], (times, width)) for r in range(count)], axis=0
    )


def kernel(sizes, limit_value, *refs):
    (
        qe_hbm, qx_hbm, kt_hbm, kx_hbm, vt_hbm, vx_hbm, qc_hbm, kc_hbm, sinks, rot_hbm, do_hbm,
        g_s, gk_s, gv_s, gr_s, gs_s,
        q_s, d_s, mq_s, qx_s, kt_s, kx_s, vt_s, vx_s, qc_s, kc_s, rot_s,
        scale_s, kv_t, k_row, v_row, dk_s, dv_s, d2_s, w_s, rb_s, part_s, sinkacc, tri_s, back_in, back_in_v,
        buf_a1, buf_b1, buf_a2, buf_b2, sq_buf,
        q_sem, d_sem, in_sem, halo_sem, back_sem,
        a1_send, a1_recv, b1_send, b1_recv, a2_send, a2_recv, b2_send, b2_recv, h_send, h_recv,
    ) = refs
    nz, ny, nh, blocks, heads = sizes
    ns = nz * ny
    pairs = heads // 2
    me_s = lax.axis_index("seq")
    me_h = lax.axis_index("head")
    me_z, me_y = me_s // ny, lax.rem(me_s, ny)
    nxt, prv = lax.rem(me_s + 1, ns), lax.rem(me_s + ns - 1, ns)

    def seq_dev(s):
        return (s, me_h)

    def far_first(n):
        return sorted(range(1, n), key=lambda k: -min(k, n - k))

    z_peers = [lax.rem(me_z + k, nz) for k in far_first(nz)]
    y_peers = [lax.rem(me_y + k, ny) for k in far_first(ny)]
    chips = nh // 2
    me_x, me_c = me_h // 2, lax.rem(me_h, 2)
    steps = [(k, other) for k in far_first(chips) + [0] for other in (1, 0) if k or other]
    h_peers = [2 * lax.rem(me_x + k, chips) + (1 - me_c if other else me_c) for k, other in steps]

    barrier = pltpu.get_barrier_semaphore()
    targets = [(nxt, me_h), (prv, me_h)]
    targets += [(z * ny + me_y, me_h) for z in z_peers]
    targets += [(me_z * ny + y, me_h) for y in y_peers]
    targets += [(me_s, h) for h in h_peers]
    for dev in targets:
        pl.semaphore_signal(barrier, inc=1, device_id=dev, device_id_type=MESH)

    small = [
        (kt_hbm, kt_s), (kx_hbm, kx_s), (vt_hbm, vt_s), (vx_hbm, vx_s),
        (qx_hbm, qx_s), (qc_hbm, qc_s), (kc_hbm, kc_s), (rot_hbm, rot_s),
    ]
    small_copies = [pltpu.make_async_copy(a, b, in_sem.at[n]) for n, (a, b) in enumerate(small)]
    for c in small_copies[:4]:
        c.start()

    def q_copy(b):
        rows = pl.ds(pl.multiple_of(b * WINDOW, WINDOW), WINDOW)
        return pltpu.make_async_copy(qe_hbm.at[rows], q_s.at[rows], q_sem.at[b])

    def d_copy(b):
        rows = pl.ds(pl.multiple_of(b * WINDOW, WINDOW), WINDOW)
        return pltpu.make_async_copy(do_hbm.at[rows], d_s.at[rows], d_sem.at[b])

    for n in range(blocks):
        b = [1, 2, 3, 4, 0, 5, 6, 7][n]
        q_copy(b).start()
        d_copy(b).start()
        if n == 0:
            for c in small_copies[4:]:
                c.start()

    p_iota = lax.broadcasted_iota(jnp.int32, (WINDOW, 2 * WINDOW), 0)
    i_iota = lax.rem(lax.broadcasted_iota(jnp.int32, (WINDOW, 2 * WINDOW), 1), WINDOW)
    tri_s[...] = jnp.where(p_iota <= i_iota, 1.0, 0.0).astype(bf16)
    part_s[...] = jnp.zeros_like(part_s)
    sinkacc[...] = jnp.zeros_like(sinkacc)
    dk_s[...] = jnp.zeros_like(dk_s)
    dv_s[...] = jnp.zeros_like(dv_s)

    for c in small_copies[:4]:
        c.wait()
    ksc = jnp.exp2(kx_s[...].astype(f32)) * temper
    vsc = jnp.exp2(vx_s[...].astype(f32))
    for half in range(2):
        rr = slice(32 * half, 32 * half + 32)
        k8 = (kt_s[rr, :].astype(f32) * ksc[half : half + 1, :]).astype(bf16)
        vv = (vt_s[rr, :].astype(f32) * vsc[half : half + 1, :]).astype(bf16)
        kv_t[32 * half : 32 * half + 32, WINDOW:] = k8
        kv_t[HEAD + 32 * half : HEAD + 32 * half + 32, WINDOW:] = vv

    def rows_of(cb):
        at = pl.ds(pl.multiple_of(cb * WINDOW, WINDOW), WINDOW)
        both = kv_t[:, at]
        k_row[at, :] = both[:HEAD].T
        v_row[at, :] = both[HEAD:].T

    def rows_step(cb, carry):
        rows_of(cb)
        return carry

    lax.fori_loop(1, blocks + 1, rows_step, 0, unroll=True)

    for c in small_copies[4:]:
        c.wait()
    scale_s[...] = jnp.exp2(qx_s[...].astype(f32))
    rlow = rot_s[...].astype(bf16)
    rlow_t = rot_s[...].T.astype(bf16)
    zero = jnp.zeros((HEAD, HEAD), bf16)
    rb_s[...] = jnp.concatenate(
        [jnp.concatenate([rlow_t, zero], axis=1), jnp.concatenate([zero, rlow_t], axis=1)], axis=0
    )

    halo = pltpu.make_async_remote_copy(
        src_ref=kv_t.at[:, pl.ds(blocks * WINDOW, WINDOW)],
        dst_ref=kv_t.at[:, pl.ds(0, WINDOW)],
        send_sem=halo_sem.at[0], recv_sem=halo_sem.at[1],
        device_id=(nxt, me_h), device_id_type=MESH,
    )
    back = pltpu.make_async_remote_copy(
        src_ref=dk_s.at[:, pl.ds(0, WINDOW)],
        dst_ref=back_in,
        send_sem=back_sem.at[0], recv_sem=back_sem.at[1],
        device_id=(prv, me_h), device_id_type=MESH,
    )
    back_v = pltpu.make_async_remote_copy(
        src_ref=dv_s.at[:, pl.ds(0, WINDOW)],
        dst_ref=back_in_v,
        send_sem=back_sem.at[2], recv_sem=back_sem.at[3],
        device_id=(prv, me_h), device_id_type=MESH,
    )
    bits = jnp.left_shift(1, lax.broadcasted_iota(jnp.int32, (16, WINDOW), 0))
    bits64 = jnp.concatenate([bits] * 4, axis=0)

    sink_rows = [
        jnp.concatenate([jnp.full((1, WINDOW), sinks[2 * pr + h], f32) for h in range(2)], axis=1)
        for pr in range(pairs)
    ]

    ahead = lax.rem(lax.broadcasted_iota(jnp.int32, (8, 2 * WINDOW), 1), WINDOW) - lax.broadcasted_iota(
        jnp.int32, (8, 2 * WINDOW), 0
    )

    def step(n, carry):
        @pl.when(n == 0)
        def _():
            pl.semaphore_wait(barrier, len(targets))
            halo.start()

        @pl.when(n == 2)
        def _():
            halo.wait()
            rows_of(0)

        both = [2 * n + 1 - jnp.where(n == 2, 5, 0) + jnp.where(n == 3, -1, 0), 2 * n + 2 - jnp.where(n >= 2, 1, 0)]
        views = []
        for b in both:
            q_copy(b).wait()
            d_copy(b).wait()
            cols = pl.ds(pl.multiple_of(b * WINDOW, WINDOW), WINDOW)
            wide = pl.ds(pl.multiple_of(b * WINDOW, WINDOW), 2 * WINDOW)
            views.append((b, cols, wide))
        hidden = jnp.where((both[0] == 0) & (me_s == 0), negative, 0.0)
        trib = tri_s[...]
        units = [(k, pr) for k in range(2) for pr in range(pairs)]
        hold = {}

        def choose(now, past):
            return jnp.concatenate(
                [jnp.where(ahead >= r, now[r : r + 8], past[r : r + 8]) for r in range(0, WINDOW, 8)], axis=0
            )

        def stage_a(k, pr):
            b, cols, wide = views[k]
            lanes = slice(pr * PAIR, (pr + 1) * PAIR)
            qt = q_s[cols, lanes].T * spread(scale_s, 4 * pr, 4, 32, cols).astype(bf16)
            dt = d_s[cols, lanes].T
            q2 = jnp.concatenate([qt[:HEAD], qt[HEAD:]], axis=1)
            d2 = jnp.concatenate([dt[:HEAD], dt[HEAD:]], axis=1)
            d2_s[b, :, 2 * pr * WINDOW : 2 * (pr + 1) * WINDOW] = d2
            s_all = mm(k_row[wide, :], q2)
            before = s_all[:WINDOW] + hidden if k == 0 else s_all[:WINDOW]
            s = choose(s_all[WINDOW:], before)
            dp_all = mm(v_row[wide, :], d2)
            dp = choose(dp_all[WINDOW:], dp_all[:WINDOW])
            hold[k, pr] = (q2, s, dp)

        def stage_b(k, pr):
            b, cols, wide = views[k]
            q2, s, dp = hold[k, pr]
            sink = sink_rows[pr]
            top = jnp.maximum(jnp.max(s, axis=0, keepdims=True), sink)
            e = jnp.exp(s - top)
            es = jnp.exp(sink - top)
            inv = 1.0 / (jnp.sum(e, axis=0, keepdims=True) + es)
            w = e * inv
            t = w * dp
            delta = jnp.sum(t, axis=0, keepdims=True)
            ds = t - w * delta
            sk = es * inv * delta
            sinkacc[2 * pr : 2 * pr + 1, :] -= sk[:, :WINDOW]
            sinkacc[2 * pr + 1 : 2 * pr + 2, :] -= sk[:, WINDOW:]
            w_s[b, :, 2 * pr * WINDOW : 2 * (pr + 1) * WINDOW] = w.astype(bf16)
            sb = ds.astype(bf16)
            s_cur = sb * trib
            hold[k, pr] = (q2, jnp.concatenate([sb - s_cur, s_cur], axis=0))

        def stage_c(k, pr):
            b, cols, wide = views[k]
            q2, s2 = hold[k, pr]
            gqt = mm(kv_t[:HEAD, wide], s2)
            dk = mm(q2, s2, NT)
            dks[k] = dk if dks[k] is None else dks[k] + dk
            hold[k, pr] = (q2, gqt)

        def stage_d(k, pr):
            b, cols, wide = views[k]
            lanes = slice(pr * PAIR, (pr + 1) * PAIR)
            q2, gqt = hold.pop((k, pr))
            m2 = []
            for h in range(2):
                words = spread(qc_s, 4 * (2 * pr + h), 4, 16, cols)
                keep = jnp.bitwise_and(words, bits64) != 0
                m2.append(jnp.where(keep, gqt[:, h * WINDOW : (h + 1) * WINDOW], 0.0).astype(bf16))
            mq_s[lanes, cols] = jnp.concatenate(m2, axis=0)
            part = mm(q2, jnp.concatenate(m2, axis=1), NT)
            parts[0] = part if parts[0] is None else parts[0] + part

        dks = [None, None]
        parts = [None]
        for t in range(len(units) + LAGS[2]):
            for lag, stage in zip((0,) + LAGS, (stage_a, stage_b, stage_c, stage_d)):
                if 0 <= t - lag < len(units):
                    stage(*units[t - lag])
        for (b, cols, wide), dk in zip(views, dks):
            dk_s[:, wide] += dk
        part_s[...] += parts[0]

        @pl.when(n == 2)
        def _():
            back.start()

        return carry

    lax.fori_loop(0, blocks // 2, step, 0)
    last = pl.ds(blocks * WINDOW, WINDOW)

    def key_part(first, count):
        width = count * WINDOW
        at, ext = slice(first * WINDOW, first * WINDOW + width), slice((first + 1) * WINDOW, (first + 1) * WINDOW + width)
        words = jnp.concatenate([jnp.broadcast_to(kc_s[r : r + 1, at], (16, width)) for r in range(4)], axis=0)
        flags = jnp.left_shift(1, lax.rem(lax.broadcasted_iota(jnp.int32, (HEAD, width), 0), 16))
        mk = jnp.where(jnp.bitwise_and(words, flags) != 0, dk_s[:, ext] * temper, 0.0).astype(bf16)
        gk_s[:, at] = mk
        return mm(kv_t[:HEAD, ext], mk, NT) * (1.0 / temper)

    part = part_s[...] + key_part(0, blocks - 1)
    back.wait()
    dk_s[:, last] += back_in[...]
    part = part + key_part(blocks - 1, 1)

    cut = buf_a1.shape[1]
    folded = jnp.concatenate([part[: HEAD // 2], part[HEAD // 2 :]], axis=1)
    buf_a1[pl.ds(me_z, 1)] = folded[:cut].astype(bf16)[None]
    buf_b1[pl.ds(me_y, 1)] = (
        jnp.concatenate([folded[cut:], sinkacc[...], jnp.zeros_like(sinkacc)], axis=0).astype(bf16)[None]
    )

    def exchange(buf, me, peers, device, send, recv):
        copies = []
        for k, peer in enumerate(peers):
            copies.append(
                pltpu.make_async_remote_copy(
                    src_ref=buf.at[me], dst_ref=buf.at[me],
                    send_sem=send.at[k], recv_sem=recv.at[k],
                    device_id=device(peer), device_id_type=MESH,
                )
            )
        for c in copies:
            c.start()
        return copies

    def along_z(z):
        return (z * ny + me_y, me_h)

    def along_y(y):
        return (me_z * ny + y, me_h)

    def along_h(h):
        return (me_s, h)

    def total(buf, count):
        acc = buf[0].astype(f32)
        for k in range(1, count):
            acc = acc + buf[k].astype(f32)
        return acc

    copies_b = first_b = exchange(buf_b1, me_y, y_peers, along_y, b1_send, b1_recv)
    copies_a = first_a = exchange(buf_a1, me_z, z_peers, along_z, a1_send, a1_recv)

    def turn(b, carry):
        cols = pl.ds(pl.multiple_of(b * WINDOW, WINDOW), WINDOW)
        for pr in range(pairs):
            lanes = slice(pr * PAIR, (pr + 1) * PAIR)
            g_s[cols, lanes] = mm(mq_s[lanes, cols].T, rb_s[...]).astype(bf16)
        return carry

    def values(b, carry):
        wide = pl.ds(pl.multiple_of(b * WINDOW, WINDOW), 2 * WINDOW)
        wb = w_s[b]
        w_cur = wb * jnp.concatenate([tri_s[...]] * pairs, axis=1)
        dv_s[:, wide] += mm(d2_s[b], jnp.concatenate([wb - w_cur, w_cur], axis=0), NT)
        return carry

    values(0, 0)
    back_v.start()
    lax.fori_loop(1, blocks, values, 0)
    for c in copies_a:
        c.wait_recv()
    buf_a2[pl.ds(me_y, 1)] = total(buf_a1, nz).astype(bf16)[None]
    copies_a = exchange(buf_a2, me_y, y_peers, along_y, a2_send, a2_recv)
    for c in copies_b:
        c.wait_recv()
    buf_b2[pl.ds(me_z, 1)] = total(buf_b1, ny).astype(bf16)[None]
    copies_b = exchange(buf_b2, me_z, z_peers, along_z, b2_send, b2_recv)
    lax.fori_loop(0, blocks, turn, 0)
    for c in copies_a:
        c.wait_recv()
    for c in copies_b:
        c.wait_recv()
    tot_a = total(buf_a2, ny)
    tot_b = total(buf_b2, nz)
    rows_b = HEAD // 2 - cut
    whole = jnp.concatenate([tot_a, tot_b[:rows_b]], axis=0)
    summed = jnp.concatenate([whole[:, :HEAD], whole[:, HEAD:]], axis=0)
    raw = lax.dot_general(
        rot_s[...], summed, NN, precision=lax.Precision.HIGHEST, preferred_element_type=f32
    )
    sq = jnp.sum(jnp.sum(raw * raw, axis=0, keepdims=True), axis=1, keepdims=True)
    sq_buf[pl.ds(me_h, 1)] = jnp.broadcast_to(sq, (1, 128))[None]
    copies_h = exchange(sq_buf, me_h, h_peers, along_h, h_send, h_recv)
    gs_s[...] = jnp.sum(tot_b[rows_b : rows_b + heads].T, axis=0, keepdims=True)
    gk_s[...] = mm(rlow, gk_s[...]).astype(bf16)
    back_v.wait()
    dv_s[:, last] += back_in_v[...]
    gv_s[...] = dv_s[:, WINDOW:].astype(bf16)
    for c in first_a + first_b + copies_a + copies_b + copies_h:
        c.wait_send()
    for c in copies_h:
        c.wait_recv()
    norm = jnp.sqrt(total(sq_buf, nh)[:1, :HEAD])
    gr_s[...] = raw * (clip_scale / jnp.maximum(norm, limit_value))


def store(*refs):
    srcs, dsts, sems = refs[:5], refs[5:10], refs[10]
    share = srcs[0].shape[0] // SHARES
    parts = [(n, None) for n in (4, 3, 2, 1)] + [(0, pl.ds(n * share, share)) for n in range(SHARES)]

    def view(ref, rows):
        return ref if rows is None else ref.at[rows]

    copies = [
        pltpu.make_async_copy(view(srcs[n], rows), view(dsts[n], rows), sems.at[k])
        for k, (n, rows) in enumerate(parts)
    ]
    for c in copies:
        c.start()
    for c in copies:
        c.wait()


def per_device(split, ns, nh, qe, qx, ke, kx, ve, vx, qc, kc, sinks, rot, dout):
    tokens, width = qe.shape
    heads = width // HEAD
    blocks = tokens // WINDOW
    nz, ny = split
    limit_value = limit_factor * math.sqrt(tokens * ns * heads * nh * HEAD)
    cut = 16
    rest = HEAD // 2 - cut + 16
    any_space = pl.BlockSpec(memory_space=pl.ANY)
    vmem = pltpu.VMEM
    dma = pltpu.SemaphoreType.DMA
    ext = tokens + WINDOW
    shapes = (
        jax.ShapeDtypeStruct((tokens, width), bf16),
        jax.ShapeDtypeStruct((HEAD, tokens), bf16),
        jax.ShapeDtypeStruct((HEAD, tokens), bf16),
        jax.ShapeDtypeStruct((HEAD, HEAD), f32),
        jax.ShapeDtypeStruct((1, heads), f32),
    )
    outs = pl.pallas_call(
        functools.partial(kernel, (nz, ny, nh, blocks, heads), limit_value),
        out_shape=shapes,
        in_specs=[any_space] * 8 + [pl.BlockSpec(memory_space=pltpu.SMEM)] + [any_space] * 2,
        out_specs=(pl.BlockSpec(memory_space=pltpu.VMEM),) * 5,
        scratch_shapes=[
            vmem((tokens, width), bf16),
            vmem((tokens, width), bf16),
            vmem((width, tokens), bf16),
            vmem((2 * heads, tokens), jnp.int32),
            vmem((HEAD, tokens), bf16),
            vmem((2, tokens), jnp.int32),
            vmem((HEAD, tokens), bf16),
            vmem((2, tokens), jnp.int32),
            vmem((4 * heads, tokens), jnp.int32),
            vmem((4, tokens), jnp.int32),
            vmem((HEAD, HEAD), f32),
            vmem((2 * heads, tokens), f32),
            vmem((2 * HEAD, ext), bf16),
            vmem((ext, HEAD), bf16),
            vmem((ext, HEAD), bf16),
            vmem((HEAD, ext), f32),
            vmem((HEAD, ext), f32),
            vmem((blocks, HEAD, heads * WINDOW), bf16),
            vmem((blocks, WINDOW, heads * WINDOW), bf16),
            vmem((PAIR, PAIR), bf16),
            vmem((HEAD, HEAD), f32),
            vmem((heads, WINDOW), f32),
            vmem((WINDOW, 2 * WINDOW), bf16),
            vmem((HEAD, WINDOW), f32),
            vmem((HEAD, WINDOW), f32),
            vmem((nz, cut, 128), bf16),
            vmem((ny, rest, 128), bf16),
            vmem((ny, cut, 128), bf16),
            vmem((nz, rest, 128), bf16),
            vmem((nh, 1, 128), f32),
            dma((blocks,)),
            dma((blocks,)),
            dma((8,)),
            dma((2,)),
            dma((4,)),
            dma((nz,)), dma((nz,)), dma((ny,)), dma((ny,)),
            dma((ny,)), dma((ny,)), dma((nz,)), dma((nz,)),
            dma((nh,)), dma((nh,)),
        ],
        compiler_params=pltpu.CompilerParams(
            collective_id=0, has_side_effects=True, vmem_limit_bytes=52 * 1024 * 1024
        ),
    )(*[pltpu.with_memory_space_constraint(x, pltpu.HBM) for x in (qe, qx.T, ke.T, kx.T, ve.T, vx.T, qc.T, kc.T, sinks, rot.reshape(HEAD, HEAD), dout)])
    gq, gk, gv, gr, gs = pl.pallas_call(
        store,
        out_shape=shapes,
        in_specs=[any_space] * 5,
        out_specs=(any_space,) * 5,
        scratch_shapes=[dma((SHARES + 4,))],
        compiler_params=pltpu.CompilerParams(vmem_limit_bytes=4 * 1024 * 1024),
    )(*outs)
    return (gq, gk.T, gv.T, gr[None], gs.reshape(heads))


def solution(mesh):
    ns, nh = mesh.shape["seq"], mesh.shape["head"]
    ny = 1 << ((ns.bit_length() - 1) // 2)
    seq_head = P("seq", "head")
    return jax.shard_map(
        functools.partial(per_device, (ns // ny, ny), ns, nh),
        mesh=mesh,
        in_specs=(seq_head,) * 8 + (P("head"), P("head", None, None), seq_head),
        out_specs=(seq_head, seq_head, seq_head, P("head", None, None), P("head")),
        check_vma=False,
    )
```

```python
import functools
import math

import jax
import jax.numpy as jnp
from jax import lax
from jax.experimental import pallas as pl
from jax.experimental.pallas import tpu as pltpu
from jax.sharding import PartitionSpec as P

WINDOW = 128
LAGS = (4, 8, 12)
SHARES = 1
HEAD = 64
PAIR = 2 * HEAD
clip_scale = 64.0
limit_factor = 0.05
temper = 0.125
negative = -1e30
f32 = jnp.float32
bf16 = jnp.bfloat16
MESH = pl.DeviceIdType.MESH

NN = (((1,), (0,)), ((), ()))
NT = (((1,), (1,)), ((), ()))


def mm(a, b, dims=NN):
    return lax.dot_general(a, b, dims, preferred_element_type=f32)


def spread(ref, first, count, times, cols):
    width = WINDOW
    return jnp.concatenate(
        [jnp.broadcast_to(ref[first + r : first + r + 1, cols], (times, width)) for r in range(count)], axis=0
    )


def kernel(sizes, limit_value, *refs):
    (
        qe_hbm, qx_hbm, kt_hbm, kx_hbm, vt_hbm, vx_hbm, qc_hbm, kc_hbm, sinks, rot_hbm, do_hbm,
        g_s, gk_s, gv_s, gr_s, gs_s,
        q_s, d_s, mq_s, qx_s, kt_s, kx_s, vt_s, vx_s, qc_s, kc_s, rot_s,
        scale_s, kv_t, k_row, v_row, dk_s, dv_s, d2_s, w_s, rb_s, part_s, sinkacc, tri_s, back_in, back_in_v,
        buf_a1, buf_b1, buf_a2, buf_b2, sq_buf,
        q_sem, d_sem, in_sem, halo_sem, back_sem,
        a1_send, a1_recv, b1_send, b1_recv, a2_send, a2_recv, b2_send, b2_recv, h_send, h_recv,
    ) = refs
    nz, ny, nh, blocks, heads = sizes
    ns = nz * ny
    pairs = heads // 2
    me_s = lax.axis_index("seq")
    me_h = lax.axis_index("head")
    me_z, me_y = me_s // ny, lax.rem(me_s, ny)
    nxt, prv = lax.rem(me_s + 1, ns), lax.rem(me_s + ns - 1, ns)

    def seq_dev(s):
        return (s, me_h)

    def far_first(n):
        return sorted(range(1, n), key=lambda k: -min(k, n - k))

    z_peers = [lax.rem(me_z + k, nz) for k in far_first(nz)]
    y_peers = [lax.rem(me_y + k, ny) for k in far_first(ny)]
    chips = nh // 2
    me_x, me_c = me_h // 2, lax.rem(me_h, 2)
    steps = [(k, other) for k in far_first(chips) + [0] for other in (1, 0) if k or other]
    h_peers = [2 * lax.rem(me_x + k, chips) + (1 - me_c if other else me_c) for k, other in steps]

    small = [
        (kt_hbm, kt_s), (kx_hbm, kx_s), (vt_hbm, vt_s), (vx_hbm, vx_s),
        (qx_hbm, qx_s), (qc_hbm, qc_s), (kc_hbm, kc_s), (rot_hbm, rot_s),
    ]
    small_copies = [pltpu.make_async_copy(a, b, in_sem.at[n]) for n, (a, b) in enumerate(small)]
    for c in small_copies[:4]:
        c.start()

    barrier = pltpu.get_barrier_semaphore()
    targets = []
    for k in range(max(nz, ny, nh) - 1):
        targets += [(z * ny + me_y, me_h) for z in z_peers[k : k + 1]]
        targets += [(me_z * ny + y, me_h) for y in y_peers[k : k + 1]]
        targets += [(me_s, h) for h in h_peers[k : k + 1]]
    targets += [(nxt, me_h), (prv, me_h)]
    for dev in targets:
        pl.semaphore_signal(barrier, inc=1, device_id=dev, device_id_type=MESH)

    def q_copy(b):
        rows = pl.ds(pl.multiple_of(b * WINDOW, WINDOW), WINDOW)
        return pltpu.make_async_copy(qe_hbm.at[rows], q_s.at[rows], q_sem.at[b])

    def d_copy(b):
        rows = pl.ds(pl.multiple_of(b * WINDOW, WINDOW), WINDOW)
        return pltpu.make_async_copy(do_hbm.at[rows], d_s.at[rows], d_sem.at[b])

    for n in range(blocks):
        b = [1, 2, 3, 4, 0, 5, 6, 7][n]
        q_copy(b).start()
        d_copy(b).start()
        if n == 0:
            for c in small_copies[4:]:
                c.start()

    p_iota = lax.broadcasted_iota(jnp.int32, (WINDOW, 2 * WINDOW), 0)
    i_iota = lax.rem(lax.broadcasted_iota(jnp.int32, (WINDOW, 2 * WINDOW), 1), WINDOW)
    tri_s[...] = jnp.where(p_iota <= i_iota, 1.0, 0.0).astype(bf16)
    part_s[...] = jnp.zeros_like(part_s)
    sinkacc[...] = jnp.zeros_like(sinkacc)
    dk_s[...] = jnp.zeros_like(dk_s)
    dv_s[...] = jnp.zeros_like(dv_s)

    for c in small_copies[:4]:
        c.wait()
    ksc = jnp.exp2(kx_s[...].astype(f32)) * temper
    vsc = jnp.exp2(vx_s[...].astype(f32))
    for half in range(2):
        rr = slice(32 * half, 32 * half + 32)
        k8 = (kt_s[rr, :].astype(f32) * ksc[half : half + 1, :]).astype(bf16)
        vv = (vt_s[rr, :].astype(f32) * vsc[half : half + 1, :]).astype(bf16)
        kv_t[32 * half : 32 * half + 32, WINDOW:] = k8
        kv_t[HEAD + 32 * half : HEAD + 32 * half + 32, WINDOW:] = vv

    def rows_of(cb):
        at = pl.ds(pl.multiple_of(cb * WINDOW, WINDOW), WINDOW)
        both = kv_t[:, at]
        k_row[at, :] = both[:HEAD].T
        v_row[at, :] = both[HEAD:].T

    def rows_step(cb, carry):
        rows_of(cb)
        return carry

    lax.fori_loop(1, blocks + 1, rows_step, 0, unroll=True)

    for c in small_copies[4:]:
        c.wait()
    scale_s[...] = jnp.exp2(qx_s[...].astype(f32))
    rlow = rot_s[...].astype(bf16)
    rlow_t = rot_s[...].T.astype(bf16)
    zero = jnp.zeros((HEAD, HEAD), bf16)
    rb_s[...] = jnp.concatenate(
        [jnp.concatenate([rlow_t, zero], axis=1), jnp.concatenate([zero, rlow_t], axis=1)], axis=0
    )

    halo = pltpu.make_async_remote_copy(
        src_ref=kv_t.at[:, pl.ds(blocks * WINDOW, WINDOW)],
        dst_ref=kv_t.at[:, pl.ds(0, WINDOW)],
        send_sem=halo_sem.at[0], recv_sem=halo_sem.at[1],
        device_id=(nxt, me_h), device_id_type=MESH,
    )
    back = pltpu.make_async_remote_copy(
        src_ref=dk_s.at[:, pl.ds(0, WINDOW)],
        dst_ref=back_in,
        send_sem=back_sem.at[0], recv_sem=back_sem.at[1],
        device_id=(prv, me_h), device_id_type=MESH,
    )
    back_v = pltpu.make_async_remote_copy(
        src_ref=dv_s.at[:, pl.ds(0, WINDOW)],
        dst_ref=back_in_v,
        send_sem=back_sem.at[2], recv_sem=back_sem.at[3],
        device_id=(prv, me_h), device_id_type=MESH,
    )
    bits = jnp.left_shift(1, lax.broadcasted_iota(jnp.int32, (16, WINDOW), 0))
    bits64 = jnp.concatenate([bits] * 4, axis=0)

    sink_rows = [
        jnp.concatenate([jnp.full((1, WINDOW), sinks[2 * pr + h], f32) for h in range(2)], axis=1)
        for pr in range(pairs)
    ]

    ahead = lax.rem(lax.broadcasted_iota(jnp.int32, (8, 2 * WINDOW), 1), WINDOW) - lax.broadcasted_iota(
        jnp.int32, (8, 2 * WINDOW), 0
    )

    def step(n, carry):
        @pl.when(n == 0)
        def _():
            pl.semaphore_wait(barrier, len(targets))
            halo.start()

        @pl.when(n == 2)
        def _():
            halo.wait()
            rows_of(0)

        both = [2 * n + 1 - jnp.where(n == 2, 5, 0) + jnp.where(n == 3, -1, 0), 2 * n + 2 - jnp.where(n >= 2, 1, 0)]
        views = []
        for b in both:
            q_copy(b).wait()
            d_copy(b).wait()
            cols = pl.ds(pl.multiple_of(b * WINDOW, WINDOW), WINDOW)
            wide = pl.ds(pl.multiple_of(b * WINDOW, WINDOW), 2 * WINDOW)
            views.append((b, cols, wide))
        hidden = jnp.where((both[0] == 0) & (me_s == 0), negative, 0.0)
        trib = tri_s[...]
        units = [(k, pr) for k in range(2) for pr in range(pairs)]
        hold = {}

        def choose(now, past):
            return jnp.concatenate(
                [jnp.where(ahead >= r, now[r : r + 8], past[r : r + 8]) for r in range(0, WINDOW, 8)], axis=0
            )

        def stage_a(k, pr):
            b, cols, wide = views[k]
            lanes = slice(pr * PAIR, (pr + 1) * PAIR)
            qt = q_s[cols, lanes].T * spread(scale_s, 4 * pr, 4, 32, cols).astype(bf16)
            dt = d_s[cols, lanes].T
            q2 = jnp.concatenate([qt[:HEAD], qt[HEAD:]], axis=1)
            d2 = jnp.concatenate([dt[:HEAD], dt[HEAD:]], axis=1)
            d2_s[b, :, 2 * pr * WINDOW : 2 * (pr + 1) * WINDOW] = d2
            s_all = mm(k_row[wide, :], q2)
            before = s_all[:WINDOW] + hidden if k == 0 else s_all[:WINDOW]
            s = choose(s_all[WINDOW:], before)
            dp_all = mm(v_row[wide, :], d2)
            dp = choose(dp_all[WINDOW:], dp_all[:WINDOW])
            hold[k, pr] = (q2, s, dp)

        def stage_b(k, pr):
            b, cols, wide = views[k]
            q2, s, dp = hold[k, pr]
            sink = sink_rows[pr]
            top = jnp.maximum(jnp.max(s, axis=0, keepdims=True), sink)
            e = jnp.exp(s - top)
            es = jnp.exp(sink - top)
            inv = 1.0 / (jnp.sum(e, axis=0, keepdims=True) + es)
            w = e * inv
            t = w * dp
            delta = jnp.sum(t, axis=0, keepdims=True)
            ds = t - w * delta
            sk = es * inv * delta
            sinkacc[2 * pr : 2 * pr + 1, :] -= sk[:, :WINDOW]
            sinkacc[2 * pr + 1 : 2 * pr + 2, :] -= sk[:, WINDOW:]
            w_s[b, :, 2 * pr * WINDOW : 2 * (pr + 1) * WINDOW] = w.astype(bf16)
            sb = ds.astype(bf16)
            s_cur = sb * trib
            hold[k, pr] = (q2, jnp.concatenate([sb - s_cur, s_cur], axis=0))

        def stage_c(k, pr):
            b, cols, wide = views[k]
            q2, s2 = hold[k, pr]
            gqt = mm(kv_t[:HEAD, wide], s2)
            dk = mm(q2, s2, NT)
            dks[k] = dk if dks[k] is None else dks[k] + dk
            hold[k, pr] = (q2, gqt)

        def stage_d(k, pr):
            b, cols, wide = views[k]
            lanes = slice(pr * PAIR, (pr + 1) * PAIR)
            q2, gqt = hold.pop((k, pr))
            m2 = []
            for h in range(2):
                words = spread(qc_s, 4 * (2 * pr + h), 4, 16, cols)
                keep = jnp.bitwise_and(words, bits64) != 0
                m2.append(jnp.where(keep, gqt[:, h * WINDOW : (h + 1) * WINDOW], 0.0).astype(bf16))
            mq_s[lanes, cols] = jnp.concatenate(m2, axis=0)
            part = mm(q2, jnp.concatenate(m2, axis=1), NT)
            parts[0] = part if parts[0] is None else parts[0] + part

        dks = [None, None]
        parts = [None]
        for t in range(len(units) + LAGS[2]):
            for lag, stage in zip((0,) + LAGS, (stage_a, stage_b, stage_c, stage_d)):
                if 0 <= t - lag < len(units):
                    stage(*units[t - lag])
        for (b, cols, wide), dk in zip(views, dks):
            dk_s[:, wide] += dk
        part_s[...] += parts[0]

        @pl.when(n == 2)
        def _():
            back.start()

        return carry

    lax.fori_loop(0, blocks // 2, step, 0)
    last = pl.ds(blocks * WINDOW, WINDOW)

    def key_part(first, count):
        width = count * WINDOW
        at, ext = slice(first * WINDOW, first * WINDOW + width), slice((first + 1) * WINDOW, (first + 1) * WINDOW + width)
        words = jnp.concatenate([jnp.broadcast_to(kc_s[r : r + 1, at], (16, width)) for r in range(4)], axis=0)
        flags = jnp.left_shift(1, lax.rem(lax.broadcasted_iota(jnp.int32, (HEAD, width), 0), 16))
        mk = jnp.where(jnp.bitwise_and(words, flags) != 0, dk_s[:, ext] * temper, 0.0).astype(bf16)
        gk_s[:, at] = mk
        return mm(kv_t[:HEAD, ext], mk, NT) * (1.0 / temper)

    part = part_s[...] + key_part(0, blocks - 1)
    back.wait()
    dk_s[:, last] += back_in[...]
    part = part + key_part(blocks - 1, 1)

    cut = buf_a1.shape[1]
    folded = jnp.concatenate([part[: HEAD // 2], part[HEAD // 2 :]], axis=1)
    buf_a1[pl.ds(me_z, 1)] = folded[:cut].astype(bf16)[None]
    buf_b1[pl.ds(me_y, 1)] = (
        jnp.concatenate([folded[cut:], sinkacc[...], jnp.zeros_like(sinkacc)], axis=0).astype(bf16)[None]
    )

    def exchange(buf, me, peers, device, send, recv):
        copies = []
        for k, peer in enumerate(peers):
            copies.append(
                pltpu.make_async_remote_copy(
                    src_ref=buf.at[me], dst_ref=buf.at[me],
                    send_sem=send.at[k], recv_sem=recv.at[k],
                    device_id=device(peer), device_id_type=MESH,
                )
            )
        for c in copies:
            c.start()
        return copies

    def along_z(z):
        return (z * ny + me_y, me_h)

    def along_y(y):
        return (me_z * ny + y, me_h)

    def along_h(h):
        return (me_s, h)

    def total(buf, count):
        acc = buf[0].astype(f32)
        for k in range(1, count):
            acc = acc + buf[k].astype(f32)
        return acc

    copies_b = first_b = exchange(buf_b1, me_y, y_peers, along_y, b1_send, b1_recv)
    copies_a = first_a = exchange(buf_a1, me_z, z_peers, along_z, a1_send, a1_recv)

    def turn(b, carry):
        cols = pl.ds(pl.multiple_of(b * WINDOW, WINDOW), WINDOW)
        for pr in range(pairs):
            lanes = slice(pr * PAIR, (pr + 1) * PAIR)
            g_s[cols, lanes] = mm(mq_s[lanes, cols].T, rb_s[...]).astype(bf16)
        return carry

    def values(b, carry):
        wide = pl.ds(pl.multiple_of(b * WINDOW, WINDOW), 2 * WINDOW)
        wb = w_s[b]
        w_cur = wb * jnp.concatenate([tri_s[...]] * pairs, axis=1)
        dv_s[:, wide] += mm(d2_s[b], jnp.concatenate([wb - w_cur, w_cur], axis=0), NT)
        return carry

    values(0, 0)
    back_v.start()
    lax.fori_loop(1, blocks, values, 0)
    for c in copies_a:
        c.wait_recv()
    buf_a2[pl.ds(me_y, 1)] = total(buf_a1, nz).astype(bf16)[None]
    copies_a = exchange(buf_a2, me_y, y_peers, along_y, a2_send, a2_recv)
    for c in copies_b:
        c.wait_recv()
    buf_b2[pl.ds(me_z, 1)] = total(buf_b1, ny).astype(bf16)[None]
    copies_b = exchange(buf_b2, me_z, z_peers, along_z, b2_send, b2_recv)
    lax.fori_loop(0, blocks, turn, 0)
    for c in copies_a:
        c.wait_recv()
    for c in copies_b:
        c.wait_recv()
    tot_a = total(buf_a2, ny)
    tot_b = total(buf_b2, nz)
    rows_b = HEAD // 2 - cut
    whole = jnp.concatenate([tot_a, tot_b[:rows_b]], axis=0)
    summed = jnp.concatenate([whole[:, :HEAD], whole[:, HEAD:]], axis=0)
    raw = lax.dot_general(
        rot_s[...], summed, NN, precision=lax.Precision.HIGHEST, preferred_element_type=f32
    )
    sq = jnp.sum(jnp.sum(raw * raw, axis=0, keepdims=True), axis=1, keepdims=True)
    sq_buf[pl.ds(me_h, 1)] = jnp.broadcast_to(sq, (1, 128))[None]
    copies_h = exchange(sq_buf, me_h, h_peers, along_h, h_send, h_recv)
    gs_s[...] = jnp.sum(tot_b[rows_b : rows_b + heads].T, axis=0, keepdims=True)
    gk_s[...] = mm(rlow, gk_s[...]).astype(bf16)
    back_v.wait()
    dv_s[:, last] += back_in_v[...]
    gv_s[...] = dv_s[:, WINDOW:].astype(bf16)
    for c in first_a + first_b + copies_a + copies_b + copies_h:
        c.wait_send()
    for c in copies_h:
        c.wait_recv()
    norm = jnp.sqrt(total(sq_buf, nh)[:1, :HEAD])
    gr_s[...] = raw * (clip_scale / jnp.maximum(norm, limit_value))


def store(*refs):
    srcs, dsts, sems = refs[:5], refs[5:10], refs[10]
    share = srcs[0].shape[0] // SHARES
    parts = [(n, None) for n in (4, 3, 2, 1)] + [(0, pl.ds(n * share, share)) for n in range(SHARES)]

    def view(ref, rows):
        return ref if rows is None else ref.at[rows]

    copies = [
        pltpu.make_async_copy(view(srcs[n], rows), view(dsts[n], rows), sems.at[k])
        for k, (n, rows) in enumerate(parts)
    ]
    for c in copies:
        c.start()
    for c in copies:
        c.wait()


def per_device(split, ns, nh, qe, qx, ke, kx, ve, vx, qc, kc, sinks, rot, dout):
    tokens, width = qe.shape
    heads = width // HEAD
    blocks = tokens // WINDOW
    nz, ny = split
    limit_value = limit_factor * math.sqrt(tokens * ns * heads * nh * HEAD)
    cut = 16
    rest = HEAD // 2 - cut + 16
    any_space = pl.BlockSpec(memory_space=pl.ANY)
    vmem = pltpu.VMEM
    dma = pltpu.SemaphoreType.DMA
    ext = tokens + WINDOW
    shapes = (
        jax.ShapeDtypeStruct((tokens, width), bf16),
        jax.ShapeDtypeStruct((HEAD, tokens), bf16),
        jax.ShapeDtypeStruct((HEAD, tokens), bf16),
        jax.ShapeDtypeStruct((HEAD, HEAD), f32),
        jax.ShapeDtypeStruct((1, heads), f32),
    )
    outs = pl.pallas_call(
        functools.partial(kernel, (nz, ny, nh, blocks, heads), limit_value),
        out_shape=shapes,
        in_specs=[any_space] * 8 + [pl.BlockSpec(memory_space=pltpu.SMEM)] + [any_space] * 2,
        out_specs=(pl.BlockSpec(memory_space=pltpu.VMEM),) * 5,
        scratch_shapes=[
            vmem((tokens, width), bf16),
            vmem((tokens, width), bf16),
            vmem((width, tokens), bf16),
            vmem((2 * heads, tokens), jnp.int32),
            vmem((HEAD, tokens), bf16),
            vmem((2, tokens), jnp.int32),
            vmem((HEAD, tokens), bf16),
            vmem((2, tokens), jnp.int32),
            vmem((4 * heads, tokens), jnp.int32),
            vmem((4, tokens), jnp.int32),
            vmem((HEAD, HEAD), f32),
            vmem((2 * heads, tokens), f32),
            vmem((2 * HEAD, ext), bf16),
            vmem((ext, HEAD), bf16),
            vmem((ext, HEAD), bf16),
            vmem((HEAD, ext), f32),
            vmem((HEAD, ext), f32),
            vmem((blocks, HEAD, heads * WINDOW), bf16),
            vmem((blocks, WINDOW, heads * WINDOW), bf16),
            vmem((PAIR, PAIR), bf16),
            vmem((HEAD, HEAD), f32),
            vmem((heads, WINDOW), f32),
            vmem((WINDOW, 2 * WINDOW), bf16),
            vmem((HEAD, WINDOW), f32),
            vmem((HEAD, WINDOW), f32),
            vmem((nz, cut, 128), bf16),
            vmem((ny, rest, 128), bf16),
            vmem((ny, cut, 128), bf16),
            vmem((nz, rest, 128), bf16),
            vmem((nh, 1, 128), f32),
            dma((blocks,)),
            dma((blocks,)),
            dma((8,)),
            dma((2,)),
            dma((4,)),
            dma((nz,)), dma((nz,)), dma((ny,)), dma((ny,)),
            dma((ny,)), dma((ny,)), dma((nz,)), dma((nz,)),
            dma((nh,)), dma((nh,)),
        ],
        compiler_params=pltpu.CompilerParams(
            collective_id=0, has_side_effects=True, vmem_limit_bytes=52 * 1024 * 1024
        ),
    )(*[pltpu.with_memory_space_constraint(x, pltpu.HBM) for x in (qe, qx.T, ke.T, kx.T, ve.T, vx.T, qc.T, kc.T, sinks, rot.reshape(HEAD, HEAD), dout)])
    gq, gk, gv, gr, gs = pl.pallas_call(
        store,
        out_shape=shapes,
        in_specs=[any_space] * 5,
        out_specs=(any_space,) * 5,
        scratch_shapes=[dma((SHARES + 4,))],
        compiler_params=pltpu.CompilerParams(vmem_limit_bytes=4 * 1024 * 1024),
    )(*outs)
    return (gq, gk.T, gv.T, gr[None], gs.reshape(heads))


def solution(mesh):
    ns, nh = mesh.shape["seq"], mesh.shape["head"]
    ny = 1 << ((ns.bit_length() - 1) // 2)
    seq_head = P("seq", "head")
    return jax.shard_map(
        functools.partial(per_device, (ns // ny, ny), ns, nh),
        mesh=mesh,
        in_specs=(seq_head,) * 8 + (P("head"), P("head", None, None), seq_head),
        out_specs=(seq_head, seq_head, seq_head, P("head", None, None), P("head")),
        check_vma=False,
    )
```
